32 devices in a mesh: dp: 4 (over y, core), bank: 8 (over z, x).
Axes of the slice: x: 2, y: 2, z: 4, core: 2. Of those that a mesh axis runs over, the one named last changes fastest.
Arguments:
- features: bfloat16 [64, 512, 256], P('dp', 'bank'), may hold values from -6 to 6
- patch_index: int32 [64, 128], P('dp'), may hold values from 0 to 511, as said below
- positive_index: int32 [8192], P('dp'), may hold values from 0 to 32767
- bank: bfloat16 [32768, 256], P('bank'), may hold values from -0.4 to 0.4
Outputs:
- loss: float32 [8192], P(('dp', 'bank'))
- query_grad: float32 [8192, 256], P(('dp', 'bank'))
- mean_loss: float32 [], replicated
The draws below stay inside these ranges and needn't reach their ends.
Inputs may be any that keep to these rules, and one draw needn't show every extreme that they name: `patch_index`: within one image the sampled positions are distinct.
All inputs are finite; a program needn't handle non-finite values.
Results may differ from the reference program's by a relative error of at most 0.00065.
Values may be sent and summed in bfloat16 or wider, within the bound.
No kernel may reach another device: no remote copies, remote signals or barrier semaphores. Data moves between devices by JAX's collectives and lax.ppermute only.
A program may use at most 64 MiB of HBM per device.

```python
import math
import jax
import jax.numpy as jnp
from jax import lax

C = 256
PATCHES = 128
IMAGES = 64
QUERIES = 8192
HW = 512
NB = 32768
N_BANK = 8


def draw_patch_index(key, part):
    keys = jax.random.split(jax.random.fold_in(key, 11), IMAGES)
    chosen = jax.vmap(lambda single: jax.random.permutation(single, HW)[:PATCHES])(keys)
    return chosen.astype(jnp.int32)


def draw_bank(key, part):
    key_noise, key_common, key_gain = jax.random.split(jax.random.fold_in(key, 23), 3)
    noise = jax.random.uniform(key_noise, (NB, C), jnp.float32, -1.0, 1.0)
    common = jax.random.uniform(key_common, (1, C), jnp.float32, -1.0, 1.0)
    position = jnp.arange(NB, dtype=jnp.float32)[:, None] / NB
    mixing = 0.3
    gain = jax.random.uniform(key_gain, (NB, 1), jnp.float32, 0.8, 1.2)
    scale = (1.0 + position) * gain * (math.sqrt(3.0) / 16.0)
    return (scale * (noise + mixing * common)).astype(jnp.bfloat16)


def touch_ends(drawn, key, least, top_value):
    longest = drawn.shape.index(max(drawn.shape))
    spots = []
    for shift in (0, 1):
        where = [jax.random.randint(jax.random.fold_in(key, axis), (), 0, length) for axis, length in enumerate(drawn.shape)]
        where[longest] = (where[longest] + shift) % drawn.shape[longest]
        spots.append(tuple(where))
    return drawn.at[spots[0]].set(least).at[spots[1]].set(top_value)


def block_scale(own_key, dims, cuts, low, high):
    def one(dim, shards_of):
        steps = jax.random.uniform(jax.random.fold_in(jax.random.fold_in(own_key, 6), dim), (shards_of,), jnp.float32, low / len(cuts), high / len(cuts))
        return jnp.repeat(jnp.exp(steps), dims[dim] // shards_of).reshape((-1,) + (1,) * (len(dims) - dim - 1))

    factor_of = one(*cuts[0])
    for cut in cuts[1:]:
        factor_of = factor_of * one(*cut)
    return factor_of


def bell_draw(rng, shape, spread, most, cuts=(), held_as=jnp.bfloat16):
    factor_of = block_scale(rng, shape, cuts, -0.22, 0.18) if cuts else 1.0
    drawn = jax.random.normal(rng, shape, jnp.float32) * spread * factor_of
    return jnp.minimum(jnp.maximum(drawn, -most), most).astype(held_as)


def setup_inputs(seed: int = 0) -> dict:
    streams_of = jax.random.split(jax.random.key(seed), 5)
    features = bell_draw(streams_of[0], (IMAGES, HW, C), 1.0, 6.0, ((0, 4), (1, 8)))
    patch_index = draw_patch_index(jax.random.fold_in(streams_of[4], 71), 0)
    positive_index = touch_ends(jax.random.randint(streams_of[2], (QUERIES,), 0, NB), jax.random.fold_in(streams_of[2], 1), 0, NB - 1).astype(jnp.int32)
    bank = draw_bank(jax.random.fold_in(streams_of[4], 71), 0)
    return {"features": features, "patch_index": patch_index, "positive_index": positive_index, "bank": bank}


SOFTMAX_TEMP = 0.07
EPSILON = 1e-05

def normalize(values):
    scale = lax.rsqrt(lax.optimization_barrier(jnp.mean(values * values, axis=-1, keepdims=True)) + EPSILON)
    return values * scale / math.sqrt(values.shape[-1])

def reference(features, patch_index, positive_index, bank):
    picked = jnp.take_along_axis(features, patch_index[:, :, None], axis=1)
    raw = picked.reshape(-1, picked.shape[-1]).astype(jnp.float32)
    query_vector = normalize(raw).astype(jnp.bfloat16)
    shards = bank.reshape(N_BANK, -1, bank.shape[-1])

    def visit(carry, bank_block):
        exponent_sum, weighted_negatives = carry
        logit_scores = jnp.dot(query_vector, bank_block.T, preferred_element_type=jnp.float32) / SOFTMAX_TEMP
        exponent_terms = jnp.exp(logit_scores - 1.0 / SOFTMAX_TEMP)
        exponent_sum = exponent_sum + lax.optimization_barrier(jnp.sum(exponent_terms, axis=1))
        weighted_negatives = weighted_negatives + jnp.dot(exponent_terms.astype(jnp.bfloat16), bank_block, preferred_element_type=jnp.float32)
        return ((exponent_sum, weighted_negatives), None)
    start = (jnp.zeros((raw.shape[0],), jnp.float32), jnp.zeros(raw.shape, jnp.float32))
    (exponent_sum, weighted_negatives), _ = lax.scan(visit, start, shards)
    positive_key = bank[positive_index].astype(jnp.float32)
    matched_logit = lax.optimization_barrier(jnp.sum(query_vector.astype(jnp.float32) * positive_key, axis=1)) / SOFTMAX_TEMP
    loss = jnp.log(exponent_sum) + 1.0 / SOFTMAX_TEMP - matched_logit
    query_update = (weighted_negatives / exponent_sum[:, None] - positive_key) / SOFTMAX_TEMP
    _, pullback = jax.vjp(normalize, raw)
    query_grad = pullback(query_update)[0]
    return (loss, query_grad, jnp.mean(loss))
```

```python
import functools
import math

import jax
import jax.numpy as jnp
from jax import lax
from jax.experimental import pallas as pl
from jax.experimental.pallas import tpu as pltpu
from jax.sharding import PartitionSpec as P

SOFTMAX_TEMP = 0.07
EPSILON = 1e-05
INV_TEMP = 1.0 / SOFTMAX_TEMP
STEPS = 32767.0
F32 = jnp.float32
BF16 = jnp.bfloat16
NT = (((1,), (1,)), ((), ()))
ROOM = pltpu.CompilerParams(vmem_limit_bytes=48 << 20)


def normalize(values):
    scale = lax.rsqrt(jnp.mean(values * values, axis=-1, keepdims=True) + EPSILON)
    return values * scale / math.sqrt(values.shape[-1])


def plain(features, patch_index, positive_index, bank):
    groups = lax.axis_size("bank")
    place = lax.axis_index("bank")
    images, hw_dev, channels = features.shape
    queries_dp = images * patch_index.shape[1]
    owned_rows = queries_dp // groups
    local_pos = patch_index - place * hw_dev
    onehot = (local_pos[:, :, None] == jnp.arange(hw_dev, dtype=jnp.int32)[None, None, :]).astype(BF16)
    picked = jnp.einsum("iph,ihc->ipc", onehot, features, preferred_element_type=F32)
    raw_all = lax.psum(picked.reshape(queries_dp, channels), "bank")
    query_vector = normalize(raw_all).astype(BF16)
    raw_own = lax.dynamic_slice_in_dim(raw_all, place * owned_rows, owned_rows, 0)
    bank_dev = bank.shape[0]
    block_keys = math.gcd(bank_dev, 512)

    def visit(index, carry):
        exponent_sum, weighted = carry
        block = lax.dynamic_slice_in_dim(bank, index * block_keys, block_keys, 0)
        logit = lax.dot_general(query_vector, block, NT, preferred_element_type=F32) / SOFTMAX_TEMP
        terms = jnp.exp(logit - INV_TEMP)
        exponent_sum = exponent_sum + jnp.sum(terms, axis=1)
        weighted = weighted + jnp.dot(terms.astype(BF16), block, preferred_element_type=F32)
        return (exponent_sum, weighted)

    start = (jnp.zeros((queries_dp,), F32), jnp.zeros((queries_dp, channels), F32))
    exponent_sum, weighted = lax.fori_loop(0, bank_dev // block_keys, visit, start)
    key_pos = positive_index - place * bank_dev
    inside = (key_pos >= 0) & (key_pos < bank_dev)
    rows_pos = jnp.clip(key_pos, 0, bank_dev - 1)
    positive_key = bank[rows_pos].astype(F32) * inside[:, None].astype(F32)
    matched = jnp.sum(query_vector.astype(F32) * positive_key, axis=1) / SOFTMAX_TEMP
    own_sum, own_logit, own_weighted, own_positive = (
        lax.psum_scatter(v, "bank", scatter_dimension=0, tiled=True)
        for v in (exponent_sum, matched, weighted, positive_key)
    )
    step = (own_weighted / own_sum[:, None] - own_positive) / SOFTMAX_TEMP
    loss = jnp.log(own_sum) + INV_TEMP - own_logit
    _, pullback = jax.vjp(normalize, raw_own)
    query_grad = pullback(step)[0]
    count_all = queries_dp * lax.axis_size("dp")
    mean_loss = lax.psum(jnp.sum(loss), ("dp", "bank")) / count_all
    return (loss, query_grad, mean_loss)


def capacity(mean, least, sigmas):
    room = mean + sigmas * math.sqrt(mean)
    return min(least, -(-int(math.ceil(room)) // 16) * 16)


def pick_kernel(groups, owned, cap, place_ref, pos_ref, feat_ref, own_ref, other_ref, loc_ref, most_ref):
    place = place_ref[0]
    images, patches = pos_ref.shape
    hw = feat_ref.shape[1]
    pos = pos_ref[...]
    holder = pos // hw
    row = lax.broadcasted_iota(jnp.int32, pos.shape, 0) * patches + lax.broadcasted_iota(jnp.int32, pos.shape, 1)
    parity = (row // owned) % 2
    code = holder * 2 + parity
    up = lax.broadcasted_iota(jnp.int32, (patches, patches), 0) <= lax.broadcasted_iota(
        jnp.int32, (patches, patches), 1
    )
    up = up.astype(F32).astype(BF16)
    low = lax.broadcasted_iota(jnp.int32, (images, images), 0) > lax.broadcasted_iota(
        jnp.int32, (images, images), 1
    )
    low = low.astype(F32).astype(BF16)
    ones = jnp.ones((patches, patches), BF16)
    rank = jnp.full(pos.shape, -1.0, F32)
    most = jnp.zeros((1, patches), F32)
    for g in range(2 * groups):
        hit = (code == g).astype(F32)
        mask = hit.astype(BF16)
        prefix = jnp.dot(mask, up, preferred_element_type=F32)
        count = jnp.dot(mask, ones, preferred_element_type=F32)
        before = jnp.dot(low, count.astype(BF16), preferred_element_type=F32)
        rank = rank + hit * (prefix + before)
        most = jnp.maximum(most, jnp.sum(count, axis=0, keepdims=True))
    most_ref[...] = jnp.broadcast_to(most, most_ref.shape)
    inner = place % 2
    outer = place // 2
    turns = groups // 2
    away = (outer - holder // 2 + turns) % turns
    side = (holder % 2 + inner) % 2
    ranks = rank.astype(jnp.int32)
    loc_ref[...] = (away * 2 + side) * cap + ranks
    local = pos - place * hw
    mine = holder == place
    slot = ranks + jnp.where(parity == inner, 0, cap)
    slot = jnp.where(mine & (ranks < cap), slot, -1)
    total = jnp.zeros((2 * cap, feat_ref.shape[2]), F32)
    where_slot = lax.broadcasted_iota(jnp.int32, (2 * cap, patches), 0)
    where_pos = lax.broadcasted_iota(jnp.int32, (hw, patches), 0)
    for i in range(images):
        chosen = (where_slot == slot[i : i + 1, :]).astype(F32).astype(BF16)
        spots = (where_pos == local[i : i + 1, :]).astype(F32).astype(BF16)
        table = lax.dot_general(chosen, spots, NT, preferred_element_type=F32)
        total = total + jnp.dot(table.astype(BF16), feat_ref[i], preferred_element_type=F32)
    own_ref[...] = total[:cap].astype(BF16)
    other_ref[...] = total[cap:].astype(BF16)


def pick(features, patch_index, place, groups, owned, cap):
    images, patches = patch_index.shape
    channels = features.shape[2]
    return pl.pallas_call(
        functools.partial(pick_kernel, groups, owned, cap),
        in_specs=[
            pl.BlockSpec(memory_space=pltpu.SMEM),
            pl.BlockSpec(memory_space=pltpu.VMEM),
            pl.BlockSpec(memory_space=pltpu.VMEM),
        ],
        out_specs=[pl.BlockSpec(memory_space=pltpu.VMEM)] * 4,
        out_shape=[
            jax.ShapeDtypeStruct((cap, channels), BF16),
            jax.ShapeDtypeStruct((cap, channels), BF16),
            jax.ShapeDtypeStruct((images, patches), jnp.int32),
            jax.ShapeDtypeStruct((8, patches), F32),
        ],
        compiler_params=ROOM,
        cost_estimate=pl.CostEstimate(flops=10**9, bytes_accessed=10**6, transcendentals=0),
        name="pick",
    )(place.reshape(1), patch_index, features)


def arrange_kernel(cap, loc_ref, *refs):
    query_ref, raw_ref = refs[-2:]
    rows = loc_ref.shape[0]
    loc = loc_ref[...]
    lane = lax.broadcasted_iota(jnp.int32, (rows, cap), 1)
    raw = jnp.zeros(query_ref.shape, F32)
    for b, ref in enumerate(refs[:-2]):
        table = (lane + b * cap == loc).astype(F32).astype(BF16)
        raw = raw + jnp.dot(table, ref[...], preferred_element_type=F32)
    raw_ref[...] = raw.astype(BF16)
    query_ref[...] = normalize(raw).astype(BF16)


def arrange(loc, parts, cap):
    rows = loc.shape[0]
    channels = parts[0].shape[1]
    block = math.gcd(rows, 256)
    whole = pl.BlockSpec((cap, channels), lambda i: (0, 0))
    tall = pl.BlockSpec((block, channels), lambda i: (i, 0))
    return pl.pallas_call(
        functools.partial(arrange_kernel, cap),
        grid=(rows // block,),
        in_specs=[pl.BlockSpec((block, 1), lambda i: (i, 0))] + [whole] * len(parts),
        out_specs=[tall, tall],
        out_shape=[jax.ShapeDtypeStruct((rows, channels), BF16)] * 2,
        compiler_params=ROOM,
        cost_estimate=pl.CostEstimate(
            flops=2 * rows * cap * len(parts) * channels, bytes_accessed=3 * rows * channels, transcendentals=0
        ),
        name="arrange",
    )(loc, *parts)


def sweep(query, keys, sub, total, pushed):
    for at in range(0, keys.shape[0], sub):
        block = keys[at : at + sub, :]
        logit = lax.dot_general(query, block, NT, preferred_element_type=F32)
        terms = jnp.exp(logit * INV_TEMP - INV_TEMP)
        for c in range(0, sub, 128):
            total = total + terms[:, c : c + 128]
        pushed = pushed + jnp.dot(terms.astype(BF16), block, preferred_element_type=F32)
    return total, pushed


def first_kernel(sub, query_ref, keys_ref, total_ref, pushed_ref):
    total, pushed = sweep(
        query_ref[...], keys_ref, sub, jnp.zeros(total_ref.shape, F32), jnp.zeros(pushed_ref.shape, F32)
    )
    total_ref[...] = total
    pushed_ref[...] = pushed


def flash_cost(rows, keys, channels):
    return pl.CostEstimate(
        flops=4 * rows * keys * channels, bytes_accessed=2 * (rows + keys) * channels, transcendentals=rows * keys
    )


def first(query, keys):
    rows, channels = query.shape
    return pl.pallas_call(
        functools.partial(first_kernel, math.gcd(keys.shape[0], 256)),
        in_specs=[pl.BlockSpec(memory_space=pltpu.VMEM)] * 2,
        out_specs=[pl.BlockSpec(memory_space=pltpu.VMEM)] * 2,
        out_shape=[jax.ShapeDtypeStruct((rows, 128), F32), jax.ShapeDtypeStruct((rows, channels), F32)],
        compiler_params=ROOM,
        cost_estimate=flash_cost(rows, keys.shape[0], channels),
        name="first",
    )(query, keys)


def last_kernel(count, coded, query_ref, total_in, pushed_in, *refs):
    key_refs = refs[:count]
    pushed_ref, stats_ref = refs[count:]
    query = query_ref[...]
    total, pushed = total_in[...], pushed_in[...]
    for ref in key_refs:
        total, pushed = sweep(query, ref, math.gcd(ref.shape[0], 256), total, pushed)
    stats_ref[0:1, :] = jnp.sum(total.T, axis=0, keepdims=True)
    if not coded:
        pushed_ref[...] = pushed
        stats_ref[1:2, :] = jnp.zeros((1, stats_ref.shape[1]), F32)
        return
    size = jnp.abs(pushed)
    wide = size[:, :128]
    for c in range(128, size.shape[1], 128):
        wide = jnp.maximum(wide, size[:, c : c + 128])
    top = jnp.maximum(jnp.max(wide, axis=1, keepdims=True), 1e-30)
    stats_ref[1:2, :] = jnp.maximum(jnp.max(wide.T, axis=0, keepdims=True), 1e-30)
    pushed_ref[...] = jnp.round(pushed * (STEPS / top)).astype(jnp.int32).astype(jnp.int16)


def last(query, total, pushed, keys, start, rows, coded):
    channels = query.shape[1]
    at = start // rows
    part = lambda width: pl.BlockSpec((rows, width), lambda i: (at, 0))
    return pl.pallas_call(
        functools.partial(last_kernel, len(keys), coded),
        grid=(1,),
        in_specs=[part(channels), part(128), part(channels)]
        + [pl.BlockSpec(k.shape, lambda i: (0, 0)) for k in keys],
        out_specs=[pl.BlockSpec((rows, channels), lambda i: (0, 0)), pl.BlockSpec((2, rows), lambda i: (0, 0))],
        out_shape=[
            jax.ShapeDtypeStruct((rows, channels), jnp.int16 if coded else F32),
            jax.ShapeDtypeStruct((2, rows), F32),
        ],
        compiler_params=ROOM,
        cost_estimate=flash_cost(rows, sum(k.shape[0] for k in keys), channels),
        name="last",
    )(query, total, pushed, *keys)


def finish_kernel(count, raw_ref, positive_ref, own_ref, stats_ref, *refs):
    grad_ref = refs[-1]
    rows = raw_ref.shape[0]
    turned = jnp.concatenate(
        [stats_ref[...], jnp.zeros((128 - stats_ref.shape[0], rows), F32)], axis=0
    ).T
    pushed = own_ref[...]
    for j in range(count):
        pushed = pushed + refs[j][...].astype(jnp.int32).astype(F32) * (turned[:, j + 1 : j + 2] * (1.0 / STEPS))
    step = (pushed / turned[:, 0:1] - positive_ref[...].astype(F32)) * INV_TEMP
    raw = raw_ref[...].astype(F32)
    scale = lax.rsqrt(jnp.mean(raw * raw, axis=-1, keepdims=True) + EPSILON)
    inner = jnp.mean(step * raw, axis=-1, keepdims=True)
    grad_ref[...] = (step - raw * (scale * scale * inner)) * (scale / math.sqrt(raw.shape[1]))


def finish(raw, positive, own, stats, parts):
    return pl.pallas_call(
        functools.partial(finish_kernel, len(parts)),
        in_specs=[pl.BlockSpec(memory_space=pltpu.VMEM)] * (4 + len(parts)),
        out_specs=pl.BlockSpec(memory_space=pltpu.VMEM),
        out_shape=jax.ShapeDtypeStruct(own.shape, F32),
        compiler_params=ROOM,
        name="finish",
    )(raw, positive, own, stats, *parts)


def on_device(features, patch_index, positive_index, bank):
    groups, copies = lax.axis_size("bank"), lax.axis_size("dp")
    place = lax.axis_index("bank")
    core = lax.axis_index("dp") % 2
    images, hw_dev, channels = features.shape
    queries_dp = images * patch_index.shape[1]
    owned = queries_dp // groups
    turns = groups // 2
    inner, outer = place % 2, place // 2
    bank_dev = bank.shape[0]
    across = [(b, b ^ 1) for b in range(groups)]
    swap = [(c, c ^ 1) for c in range(copies)]

    def turn(value, k):
        pairs = [(b, ((b // 2 + k) % turns) * 2 + b % 2) for b in range(groups)]
        return lax.ppermute(value, "bank", pairs)

    half = bank_dev // 2
    part = math.gcd(half, 1024)
    far_keys = []
    for at in range(0, half, part):
        sent = lax.dynamic_slice_in_dim(bank, core * half + at, part, 0)
        got = lax.ppermute(sent, "bank", across)
        far_keys += [got, lax.ppermute(got, "dp", swap)]

    cap = capacity(queries_dp / groups / 2, queries_dp // 2, 4.0)
    own_set, other_set, loc, most = pick(features, patch_index, place, groups, owned, cap)
    from_side = lax.ppermute(other_set, "bank", across)
    parts = [own_set, from_side]
    for k in range(1, turns):
        parts += [turn(own_set, k), turn(from_side, k)]
    loc = lax.dynamic_index_in_dim(loc.reshape(turns, 2, owned), inner, 1, keepdims=False)
    loc = lax.dynamic_slice_in_dim(jnp.concatenate([loc, loc]), outer, turns, 0)
    query, raw = arrange(loc.reshape(turns * owned, 1), parts, cap)

    cap_pos = capacity(owned / groups, owned, 5.5)
    index = positive_index.reshape(groups, owned)
    holder = index // bank_dev
    mine = holder == place
    order = jnp.arange(owned, dtype=jnp.int32)
    earlier = order[None, :] < order[:, None]
    rank = jnp.sum((mine[:, None, :] & earlier).astype(jnp.int32), axis=2)
    slots = jnp.arange(cap_pos, dtype=jnp.int32)
    chosen = mine[:, None, :] & (rank[:, None, :] == slots[None, :, None])
    listed = jnp.sum(jnp.where(chosen, (index - place * bank_dev)[:, None, :], 0), axis=2)
    rows_out = bank[listed.reshape(-1)].reshape(turns, 2, cap_pos, channels)
    to_me = lax.dynamic_index_in_dim(rows_out, inner, 1, keepdims=False)
    to_side = lax.dynamic_index_in_dim(rows_out, 1 - inner, 1, keepdims=False)
    side_rows = lax.ppermute(to_side, "bank", across)
    both = jnp.stack([to_me, side_rows], axis=1)
    both = lax.dynamic_slice_in_dim(jnp.concatenate([both, both]), outer, turns, 0)
    landed = jnp.stack([both[0]] + [turn(both[k], k) for k in range(1, turns)])
    landed = landed.reshape(groups * cap_pos, channels)
    own_holder = lax.dynamic_index_in_dim(holder, place, 0, keepdims=False)
    same = own_holder[None, :] == own_holder[:, None]
    own_rank = jnp.sum((same & earlier).astype(jnp.int32), axis=1)
    away = (outer - own_holder // 2 + turns) % turns
    spot = (away * 2 + (own_holder + inner) % 2) * cap_pos + own_rank
    table = (spot[:, None] == jnp.arange(groups * cap_pos, dtype=jnp.int32)[None, :]).astype(BF16)
    positive = jnp.dot(table, landed, preferred_element_type=F32)
    matched = jnp.sum(query[:owned].astype(F32) * positive, axis=1) / SOFTMAX_TEMP

    held = jnp.sum((holder[:, None, :] == jnp.arange(groups, dtype=jnp.int32)[None, :, None]).astype(jnp.int32), axis=2)
    over = (jnp.max(most) > cap) | (jnp.max(held) > cap_pos)

    total, pushed = first(query, bank)
    sent, stats = [None] * turns, [None] * turns
    moved = []
    for k in list(range(1, turns)) + [0]:
        sent[k], stats[k] = last(query, total, pushed, far_keys, k * owned, owned, k > 0)
        if k:
            moved.append(turn(sent[k], k))
    note = jnp.concatenate(
        [s[0:1] for s in stats] + [s[1:2] for s in stats] + [jnp.full((1, owned), jnp.sum(matched))]
    )
    totals = note[:turns]
    matched_line = note[2 * turns, 0]
    sizes = []
    for k in range(1, turns):
        came = turn(note, k)
        totals = totals + jnp.roll(came[:turns], -k, axis=0)
        sizes.append(came[turns + k][None])
        matched_line = matched_line + came[2 * turns, 0]
    grad = finish(raw[:owned], positive, sent[0], jnp.concatenate([totals[:1]] + sizes), moved)
    loss = jnp.log(totals[0]) + INV_TEMP - matched

    line = jnp.sum(jnp.log(totals)) + INV_TEMP * totals.size - matched_line
    word = jnp.stack([jnp.full((128,), line), jnp.full((128,), over.astype(F32))])
    everyone = word
    for a in range(copies):
        for b in range(2):
            if a or b:
                pairs = [
                    (c * groups + p, ((c + a) % copies) * groups + (p ^ b))
                    for c in range(copies)
                    for p in range(groups)
                ]
                everyone = everyone + lax.ppermute(word, ("dp", "bank"), pairs)
    mean_loss = everyone[0, 0] / (queries_dp * copies)
    return lax.cond(
        everyone[1, 0] > 0.5,
        lambda *a: plain(*a[:4]),
        lambda *a: a[4:],
        features,
        patch_index,
        positive_index,
        bank,
        loss,
        grad,
        mean_loss,
    )


def solution(mesh):
    in_specs = (P("dp", "bank", None), P("dp", None), P("dp"), P("bank", None))
    out_specs = (P(("dp", "bank")), P(("dp", "bank"), None), P())
    paired = mesh.shape["bank"] % 2 == 0 and mesh.shape["dp"] % 2 == 0
    return jax.shard_map(
        on_device if paired else plain, mesh=mesh, in_specs=in_specs, out_specs=out_specs, check_vma=False
    )
```

```python
import functools
import math

import jax
import jax.numpy as jnp
from jax import lax
from jax.experimental import pallas as pl
from jax.experimental.pallas import tpu as pltpu
from jax.sharding import PartitionSpec as P

SOFTMAX_TEMP = 0.07
EPSILON = 1e-05
INV_TEMP = 1.0 / SOFTMAX_TEMP
STEPS = 32700.0
F32 = jnp.float32
BF16 = jnp.bfloat16
NT = (((1,), (1,)), ((), ()))


def normalize(values):
    scale = lax.rsqrt(jnp.mean(values * values, axis=-1, keepdims=True) + EPSILON)
    return values * scale / math.sqrt(values.shape[-1])


def ring_sum(value, axis):
    size = lax.axis_size(axis)
    pairs = [(i, (i + 1) % size) for i in range(size)]

    def step(_, carry):
        moving, total = carry
        moving = lax.ppermute(moving, axis, pairs)
        return (moving, total + moving)

    return lax.fori_loop(0, size - 1, step, (value, value))[1]


def plain(features, patch_index, positive_index, bank):
    groups = lax.axis_size("bank")
    place = lax.axis_index("bank")
    images, hw_dev, channels = features.shape
    queries_dp = images * patch_index.shape[1]
    owned_rows = queries_dp // groups
    local_pos = patch_index - place * hw_dev
    onehot = (local_pos[:, :, None] == jnp.arange(hw_dev, dtype=jnp.int32)[None, None, :]).astype(BF16)
    picked = jnp.einsum("iph,ihc->ipc", onehot, features, preferred_element_type=F32)
    raw_all = ring_sum(picked.reshape(queries_dp, channels), "bank")
    query_vector = normalize(raw_all).astype(BF16)
    raw_own = lax.dynamic_slice_in_dim(raw_all, place * owned_rows, owned_rows, 0)
    bank_dev = bank.shape[0]
    block_keys = math.gcd(bank_dev, 512)

    def visit(index, carry):
        exponent_sum, weighted = carry
        block = lax.dynamic_slice_in_dim(bank, index * block_keys, block_keys, 0)
        logit = lax.dot_general(query_vector, block, NT, preferred_element_type=F32) / SOFTMAX_TEMP
        terms = jnp.exp(logit - INV_TEMP)
        exponent_sum = exponent_sum + jnp.sum(terms, axis=1)
        weighted = weighted + jnp.dot(terms.astype(BF16), block, preferred_element_type=F32)
        return (exponent_sum, weighted)

    start = (jnp.zeros((queries_dp,), F32), jnp.zeros((queries_dp, channels), F32))
    exponent_sum, weighted = lax.fori_loop(0, bank_dev // block_keys, visit, start)
    key_pos = positive_index - place * bank_dev
    inside = (key_pos >= 0) & (key_pos < bank_dev)
    rows_pos = jnp.clip(key_pos, 0, bank_dev - 1)
    positive_key = bank[rows_pos].astype(F32) * inside[:, None].astype(F32)
    matched = jnp.sum(query_vector.astype(F32) * positive_key, axis=1) / SOFTMAX_TEMP
    own_sum, own_logit, own_weighted, own_positive = (
        lax.dynamic_slice_in_dim(ring_sum(v, "bank"), place * owned_rows, owned_rows, 0)
        for v in (exponent_sum, matched, weighted, positive_key)
    )
    step = (own_weighted / own_sum[:, None] - own_positive) / SOFTMAX_TEMP
    loss = jnp.log(own_sum) + INV_TEMP - own_logit
    _, pullback = jax.vjp(normalize, raw_own)
    query_grad = pullback(step)[0]
    count_all = queries_dp * lax.axis_size("dp")
    mean_loss = ring_sum(ring_sum(jnp.full((8, 128), jnp.sum(loss)), "bank"), "dp")[0, 0] / count_all
    return (loss, query_grad, mean_loss)


def cost(flops):
    return pl.CostEstimate(flops=int(flops), bytes_accessed=1 << 20, transcendentals=0)


def capacity(mean, least, sigmas):
    room = mean + sigmas * math.sqrt(mean)
    return min(least, -(-int(math.ceil(room)) // 16) * 16)


def call(kernel, name, out_shape, flops, room=16, **more):
    params = pltpu.CompilerParams(vmem_limit_bytes=room << 20)
    return pl.pallas_call(
        kernel, out_shape=out_shape, compiler_params=params, cost_estimate=cost(flops), name=name, **more
    )


ANYWHERE = pl.BlockSpec(memory_space=pl.ANY)


def after(value, *others):
    return call(
        lambda *refs: None,
        "after",
        jax.ShapeDtypeStruct(value.shape, value.dtype),
        0,
        in_specs=[ANYWHERE] * (1 + len(others)),
        out_specs=ANYWHERE,
        input_output_aliases={0: 0},
    )(value, *others)


def in_lanes(column_parts, reduce):
    return reduce(column_parts.T, axis=0, keepdims=True)


def pick_kernel(
    groups, owned, cap, place_ref, pos_ref, feat_ref, bank_ref, own_ref, other_ref, loc_ref, most_ref, half_ref, sem
):
    half = half_ref.shape[0]
    rows = pl.ds(pl.multiple_of(place_ref[1] * half, half), half)
    fetch = pltpu.make_async_copy(bank_ref.at[rows], half_ref, sem)
    fetch.start()
    place = place_ref[0]
    images, patches = pos_ref.shape
    hw = feat_ref.shape[1]
    pos = pos_ref[...]
    holder = pos // hw
    row = lax.broadcasted_iota(jnp.int32, pos.shape, 0) * patches + lax.broadcasted_iota(jnp.int32, pos.shape, 1)
    parity = (row // owned) % 2
    code = holder * 2 + parity
    batch = math.gcd(2 * groups, 16)
    tall = batch * images
    up = lax.broadcasted_iota(jnp.int32, (patches, 2 * patches), 0) <= lax.broadcasted_iota(
        jnp.int32, (patches, 2 * patches), 1
    )
    up = up.astype(F32).astype(BF16)
    above = lax.broadcasted_iota(jnp.int32, (tall, tall), 0)
    under = lax.broadcasted_iota(jnp.int32, (tall, tall), 1)
    low = (above > under) & (above // images == under // images)
    low = low.astype(F32).astype(BF16)
    ranks = jnp.full(pos.shape, -1.0, F32)
    most = jnp.zeros((1, patches), F32)
    for g in range(0, 2 * groups, batch):
        hits = [(code == g + b).astype(F32) for b in range(batch)]
        mask = jnp.concatenate(hits, axis=0)
        sums = jnp.dot(mask.astype(BF16), up, preferred_element_type=F32)
        count = sums[:, patches:]
        rank = sums[:, :patches] + jnp.dot(low, count.astype(BF16), preferred_element_type=F32)
        rank = rank * mask
        for b in range(batch):
            ranks = ranks + rank[b * images : (b + 1) * images]
            most = jnp.maximum(most, jnp.sum(count[b * images : (b + 1) * images], axis=0, keepdims=True))
    most_ref[...] = jnp.broadcast_to(most, most_ref.shape)
    inner = place % 2
    outer = place // 2
    away = outer ^ (holder // 2)
    side = (holder % 2 + inner) % 2
    ranks = ranks.astype(jnp.int32)
    loc_ref[...] = (away * 2 + side) * cap + ranks
    local = pos - place * hw
    mine = holder == place
    slot = ranks + jnp.where(parity == inner, 0, cap)
    slot = jnp.where(mine & (ranks < cap), slot, -1)
    total = jnp.zeros((2 * cap, feat_ref.shape[2]), F32)
    where_slot = lax.broadcasted_iota(jnp.int32, (2 * cap, patches), 0)
    where_pos = lax.broadcasted_iota(jnp.int32, (hw, patches), 0)
    for i in range(images):
        chosen = (where_slot == slot[i : i + 1, :]).astype(F32).astype(BF16)
        spots = (where_pos == local[i : i + 1, :]).astype(F32).astype(BF16)
        table = lax.dot_general(chosen, spots, NT, preferred_element_type=F32)
        total = total + jnp.dot(table.astype(BF16), feat_ref[i], preferred_element_type=F32)
    own_ref[...] = total[:cap].astype(BF16)
    other_ref[...] = total[cap:].astype(BF16)
    fetch.wait()


def pick(features, patch_index, bank, place, core, groups, owned, cap):
    images, patches = patch_index.shape
    channels = features.shape[2]
    return call(
        functools.partial(pick_kernel, groups, owned, cap),
        "pick",
        [
            jax.ShapeDtypeStruct((cap, channels), BF16),
            jax.ShapeDtypeStruct((cap, channels), BF16),
            jax.ShapeDtypeStruct((images, patches), jnp.int32),
            jax.ShapeDtypeStruct((8, patches), F32),
            jax.ShapeDtypeStruct((bank.shape[0] // 2, channels), BF16),
        ],
        3e9,
        in_specs=[
            pl.BlockSpec(memory_space=pltpu.SMEM),
            pl.BlockSpec(memory_space=pltpu.VMEM),
            pl.BlockSpec(memory_space=pltpu.VMEM),
            pl.BlockSpec(memory_space=pl.ANY),
        ],
        scratch_shapes=[pltpu.SemaphoreType.DMA],
    )(jnp.stack([place, core]), patch_index, features, bank)


def pack_kernel(turns, place_ref, mine_ref, side_ref, *refs):
    cap = mine_ref.shape[2]
    outs = refs[-turns:]
    for k in range(turns):
        outer = (place_ref[0] // 2) ^ k
        outs[k][:cap, :] = mine_ref[outer, place_ref[0] % 2]
        outs[k][cap:, :] = side_ref[outer]


def pack(place, mine, side, gates):
    turns, _, cap, channels = mine.shape
    return call(
        functools.partial(pack_kernel, turns),
        "pack",
        [jax.ShapeDtypeStruct((2 * cap, channels), BF16)] * turns,
        1e8,
        in_specs=[pl.BlockSpec(memory_space=pltpu.SMEM)]
        + [pl.BlockSpec(memory_space=pltpu.VMEM)] * 2
        + [ANYWHERE] * len(gates),
    )(place.reshape(1), mine, side, *gates)


def arrange_kernel(turns, loc_ref, gate_ref, *refs):
    parts, (query_ref, raw_ref), blocks = refs[: -2 - turns], refs[-2 - turns : -turns], refs[-turns:]
    rows = loc_ref.shape[0]
    loc = loc_ref[...]
    raw = jnp.zeros(query_ref.shape, F32)
    at = 0
    for ref in parts:
        lane = lax.broadcasted_iota(jnp.int32, (rows, ref.shape[0]), 1)
        table = (lane + at == loc).astype(F32).astype(BF16)
        raw = raw + jnp.dot(table, ref[...], preferred_element_type=F32)
        at += ref.shape[0]
    query = normalize(raw).astype(BF16)
    query_ref[...] = query
    owned = raw_ref.shape[0]

    @pl.when(pl.program_id(0) == 0)
    def _():
        raw_ref[...] = raw[:owned].astype(BF16)

    each = rows // owned
    for k in range(turns):

        @pl.when(pl.program_id(0) == k // each)
        def _():
            blocks[k][...] = query[k % each * owned : (k % each + 1) * owned]


def arrange(loc, parts, owned, gate):
    rows = loc.shape[0]
    turns = rows // owned
    channels = parts[0].shape[1]
    block = max(math.gcd(rows, 256), owned)
    all_of = lambda shape: pl.BlockSpec(shape, lambda i: (0, 0))
    out = call(
        functools.partial(arrange_kernel, turns),
        "arrange",
        [jax.ShapeDtypeStruct((rows, channels), BF16)] + [jax.ShapeDtypeStruct((owned, channels), BF16)] * (turns + 1),
        2e6 * rows,
        grid=(rows // block,),
        in_specs=[pl.BlockSpec((block, 1), lambda i: (i, 0)), ANYWHERE] + [all_of(v.shape) for v in parts],
        out_specs=[pl.BlockSpec((block, channels), lambda i: (i, 0))] + [all_of((owned, channels))] * (turns + 1),
    )(loc, gate, *parts)
    return out[0], out[1], out[2:]


def match_kernel(turns, spot_ref, note_in, query_ref, *refs):
    positive_ref, matched_ref, note_ref = refs[-3:]
    rows = spot_ref.shape[0]
    landed = jnp.concatenate([ref[...] for ref in refs[:-3]], axis=0)
    table = lax.broadcasted_iota(jnp.int32, (rows, landed.shape[0]), 1) == spot_ref[...]
    positive = jnp.dot(table.astype(F32).astype(BF16), landed, preferred_element_type=F32)
    positive_ref[...] = positive.astype(BF16)
    matched = in_lanes(query_ref[...].astype(F32) * positive, jnp.sum) / SOFTMAX_TEMP
    matched_ref[...] = matched
    note_ref[...] = note_in[...]
    note_ref[turns : turns + 1, :] = matched


def match(spot, landed, query, note, turns):
    rows, channels = query.shape
    return call(
        functools.partial(match_kernel, turns),
        "match",
        [
            jax.ShapeDtypeStruct((rows, channels), BF16),
            jax.ShapeDtypeStruct((1, rows), F32),
            jax.ShapeDtypeStruct(note.shape, F32),
        ],
        3e8,
    )(spot, note, query, *landed)


def sweep(query, keys, total, pushed):
    sub = math.gcd(keys.shape[0], 512)
    for at in range(0, keys.shape[0], sub):
        block = keys[at : at + sub, :]
        logit = lax.dot_general(query, block, NT, preferred_element_type=F32)
        terms = jnp.exp(logit * INV_TEMP - INV_TEMP)
        if total is not None:
            for c in range(0, sub, 128):
                total = total + terms[:, c : c + 128]
        pushed = pushed + jnp.dot(terms.astype(BF16), block, preferred_element_type=F32)
    return total, pushed


def first_kernel(turns, gates, query_ref, keys_ref, *refs):
    total_ref, blocks = refs[gates], refs[gates + 1 :]
    query = query_ref[...]
    total, pushed = sweep(query, keys_ref, jnp.zeros(total_ref.shape, F32), jnp.zeros(query.shape, F32))
    total_ref[...] = total
    rows = query.shape[0] // turns
    for k in range(turns):
        blocks[k][...] = pushed[k * rows : (k + 1) * rows]


def first(query, keys, turns, gates):
    rows, channels = query.shape
    out = call(
        functools.partial(first_kernel, turns, len(gates)),
        "first",
        [jax.ShapeDtypeStruct((rows, 128), F32)] + [jax.ShapeDtypeStruct((rows // turns, channels), F32)] * turns,
        4 * rows * keys.shape[0] * channels,
        room=24,
        in_specs=[pl.BlockSpec(memory_space=pltpu.VMEM)] * 2 + [ANYWHERE] * len(gates),
    )(query, keys, *gates)
    return out[0], out[1:]


def lane_sums(query, keys, total):
    sub = math.gcd(keys.shape[0], 256)
    for at in range(0, keys.shape[0], sub):
        logit = lax.dot_general(query, keys[at : at + sub, :], NT, preferred_element_type=F32)
        terms = jnp.exp(logit * INV_TEMP - INV_TEMP)
        for c in range(0, sub, 128):
            total = total + terms[:, c : c + 128]
    return total


def far_kernel(count, turns, query_ref, total_in, *refs):
    note_ref = refs[-1]
    rows = note_ref.shape[1]
    total = total_in[...]
    for ref in refs[:count]:
        total = lane_sums(query_ref[...], ref, total)
    note_ref[...] = jnp.zeros(note_ref.shape, F32)
    for t in range(turns):
        note_ref[t : t + 1, :] = in_lanes(total[t * rows : (t + 1) * rows], jnp.sum)


def far_totals(query, total, keys, turns):
    lines = -(-(turns + 1) // 8) * 8
    return call(
        functools.partial(far_kernel, len(keys), turns),
        "far",
        jax.ShapeDtypeStruct((lines, query.shape[0] // turns), F32),
        2 * query.shape[0] * sum(k.shape[0] for k in keys) * query.shape[1],
        room=24,
    )(query, total, *keys)


def exponent(size):
    return jnp.ceil(jnp.log2(jnp.maximum(size, 1e-30)))


def last_kernel(k, query_ref, pushed_in, gate_ref, *refs):
    sent_ref = refs[-1]
    pushed = pushed_in[...]
    for ref in refs[:-1]:
        _, pushed = sweep(query_ref[...], ref, None, pushed)
    if k == 0:
        sent_ref[...] = pushed
        return
    size = jnp.abs(pushed)
    wide = size[:, :128]
    for c in range(128, size.shape[1], 128):
        wide = jnp.maximum(wide, size[:, c : c + 128])
    rows = pushed.shape[0]
    scale = jnp.exp2(-exponent(jnp.max(wide, axis=1, keepdims=True))) * STEPS
    sent_ref[:rows, :] = jnp.round(pushed * scale).astype(jnp.int32).astype(jnp.int16)
    power = exponent(in_lanes(wide, jnp.max)).astype(jnp.int32)
    rest = sent_ref.shape[1] - rows
    if rest:
        power = jnp.concatenate([power, jnp.zeros((1, rest), jnp.int32)], axis=1)
    sent_ref[rows:, :] = jnp.broadcast_to(power, (sent_ref.shape[0] - rows, sent_ref.shape[1])).astype(jnp.int16)


def last(query, pushed, keys, k, gate):
    rows, channels = query.shape
    sent = jax.ShapeDtypeStruct((rows + 16, channels), jnp.int16) if k else jax.ShapeDtypeStruct((rows, channels), F32)
    return call(
        functools.partial(last_kernel, k),
        "last",
        sent,
        4 * rows * sum(v.shape[0] for v in keys) * channels,
        in_specs=[pl.BlockSpec(memory_space=pltpu.VMEM)] * 2 + [ANYWHERE] + [pl.BlockSpec(memory_space=pltpu.VMEM)] * len(keys),
    )(query, pushed, gate, *keys)


def settle_kernel(turns, caps, note_ref, matched_ref, most_ref, held_ref, *refs):
    came = refs[: turns - 1]
    loss_ref, total_ref, word_ref = refs[turns - 1 :]
    totals = [note_ref[t : t + 1, :] for t in range(turns)]
    matched = note_ref[turns : turns + 1, :]
    for k in range(1, turns):
        ref = came[k - 1]
        for t in range(turns):
            totals[t] = totals[t] + ref[t ^ k : (t ^ k) + 1, :]
        matched = matched + ref[turns : turns + 1, :]
    total_ref[...] = totals[0]
    loss_ref[...] = jnp.log(totals[0]) + INV_TEMP - matched_ref[...]
    line = INV_TEMP * turns - matched
    for t in range(turns):
        line = line + jnp.log(totals[t])
    over = (jnp.max(most_ref[...]) > caps[0]) | (jnp.max(held_ref[...]) > caps[1])
    word_ref[...] = jnp.zeros(word_ref.shape, F32)
    word_ref[0:1, 0:1] = jnp.sum(line, axis=1, keepdims=True)
    word_ref[1:2, :] = jnp.full((1, word_ref.shape[1]), jnp.where(over, 1.0, 0.0))


def settle(note, matched, most, held, came, turns, caps):
    row = jax.ShapeDtypeStruct((1, note.shape[1]), F32)
    return call(
        functools.partial(settle_kernel, turns, caps),
        "settle",
        [row, row, jax.ShapeDtypeStruct((8, 128), F32)],
        1e8,
    )(note, matched, most, held, *came)


def finish_kernel(count, raw_ref, positive_ref, own_ref, total_ref, *refs):
    grad_ref = refs[-1]
    rows = raw_ref.shape[0]
    scales = [ref[rows : rows + 16, :rows].astype(jnp.int32).astype(F32)[0:1, :] for ref in refs[:count]]
    scales = [jnp.exp2(v) * (1.0 / STEPS) for v in scales]
    fill = -(1 + count) % 128
    turned = jnp.concatenate([total_ref[...]] + scales + [jnp.zeros((fill, rows), F32)], axis=0).T
    pushed = own_ref[...]
    for j in range(count):
        pushed = pushed + refs[j][:rows, :].astype(jnp.int32).astype(F32) * turned[:, j + 1 : j + 2]
    step = (pushed / turned[:, 0:1] - positive_ref[...].astype(F32)) * INV_TEMP
    raw = raw_ref[...].astype(F32)
    scale = lax.rsqrt(jnp.mean(raw * raw, axis=-1, keepdims=True) + EPSILON)
    inner = jnp.mean(step * raw, axis=-1, keepdims=True)
    grad_ref[...] = (step - raw * (scale * scale * inner)) * (scale / math.sqrt(raw.shape[1]))


def finish(raw, positive, own, total, parts):
    rows, channels = own.shape
    all_of = lambda v: pl.BlockSpec(v.shape, lambda i: (0, 0))
    return call(
        functools.partial(finish_kernel, len(parts)),
        "finish",
        jax.ShapeDtypeStruct(own.shape, F32),
        5e8,
        grid=(1,),
        in_specs=[pl.BlockSpec((rows, channels), lambda i: (0, 0))]
        + [all_of(v) for v in (positive, own, total, *parts)],
        out_specs=all_of(own),
    )(raw, positive, own, total, *parts)


def on_device(features, patch_index, positive_index, bank):
    groups, copies = lax.axis_size("bank"), lax.axis_size("dp")
    place = lax.axis_index("bank")
    core = lax.axis_index("dp") % 2
    images, hw_dev, channels = features.shape
    queries_dp = images * patch_index.shape[1]
    owned = queries_dp // groups
    turns = groups // 2
    inner, outer = place % 2, place // 2
    bank_dev = bank.shape[0]
    across = [(b, b ^ 1) for b in range(groups)]
    swap = [(c, c ^ 1) for c in range(copies)]

    def turn(value, k):
        pairs = [(b, b ^ (2 * k)) for b in range(groups)]
        return lax.ppermute(value, "bank", pairs)

    def in_turns(value):
        return [lax.dynamic_index_in_dim(value, outer ^ k, 0, keepdims=False) for k in range(turns)]

    cap = capacity(queries_dp / groups / 2, queries_dp // 2, 4.0)
    own_set, other_set, loc, most, half = pick(features, patch_index, bank, place, core, groups, owned, cap)
    from_side = lax.ppermute(other_set, "bank", across)
    fetched = lax.ppermute(half, "bank", across)
    held_rows = jnp.concatenate([own_set, from_side])
    parts = [held_rows] + [turn(held_rows, k) for k in range(1, turns)]

    cap_pos = capacity(owned / groups, owned, 5.5)
    index = positive_index.reshape(groups, owned)
    holder = index // bank_dev
    mine = holder == place
    order = jnp.arange(owned, dtype=jnp.int32)
    earlier = order[None, :] < order[:, None]
    rank = jnp.sum((mine[:, None, :] & earlier).astype(jnp.int32), axis=2)
    slots = jnp.arange(cap_pos, dtype=jnp.int32)
    chosen = mine[:, None, :] & (rank[:, None, :] == slots[None, :, None])
    listed = jnp.sum(jnp.where(chosen, (index - place * bank_dev)[:, None, :], 0), axis=2)
    rows_out = bank[after(listed, from_side).reshape(-1)].reshape(turns, 2, cap_pos, channels)
    to_side = lax.dynamic_index_in_dim(rows_out, 1 - inner, 1, keepdims=False)
    side_rows = lax.ppermute(to_side, "bank", across)

    loc = lax.dynamic_index_in_dim(loc.reshape(turns, 2, owned), inner, 1, keepdims=False)
    loc = jnp.stack(in_turns(loc)).reshape(turns * owned, 1)
    query, raw, blocks = arrange(loc, parts, owned, to_side)
    fetched = after(fetched, query)
    far_keys = [fetched, lax.ppermute(fetched, "dp", swap)]
    total, pushed = first(query, bank, turns, [])
    packed = pack(place, rows_out, side_rows, [total])
    landed = [packed[0]] + [turn(packed[k], k) for k in range(1, turns)]

    own_holder = lax.dynamic_index_in_dim(holder, place, 0, keepdims=False)
    same = own_holder[None, :] == own_holder[:, None]
    own_rank = jnp.sum((same & earlier).astype(jnp.int32), axis=1)
    away = outer ^ (own_holder // 2)
    spot = (away * 2 + (own_holder + inner) % 2) * cap_pos + own_rank
    counts = jnp.sum((holder[:, None, :] == jnp.arange(groups, dtype=jnp.int32)[None, :, None]).astype(F32), axis=2)

    note = far_totals(query, total, far_keys, turns)
    positive, matched, note = match(spot[:, None], landed, blocks[0], note, turns)

    came = [turn(note, k) for k in range(1, turns)]

    def over(word, a, b):
        pairs = [(c * groups + p, (c ^ a) * groups + (p ^ b)) for c in range(copies) for p in range(groups)]
        return lax.ppermute(word, ("dp", "bank"), pairs)

    moved = [None] * turns
    order = list(range(2, turns)) + [1]

    def send_next(gate):
        if order:
            k = order.pop(0)
            sent = last(blocks[k], pushed[k], far_keys, k, gate)
            moved[k] = turn(sent, k)

    send_next(note)
    loss, total, word = settle(note, matched, most, counts, came, turns, (cap, cap_pos))
    send_next(word)
    word = word + over(word, 1, 0)
    send_next(word)
    far_words = [over(word, a, b) for a in range(0, copies, 2) for b in range(2) if a or b]
    while order:
        send_next(word)
    own = last(blocks[0], pushed[0], far_keys, 0, word)
    moved = moved[1:]
    for far_word in far_words:
        word = word + far_word
    grad = finish(raw, positive, own, total, moved)
    mean_loss = word[0, 0] * (1.0 / (queries_dp * copies))
    return lax.cond(
        word[1, 0] > 0.5,
        lambda *a: plain(*a[:4]),
        lambda *a: a[4:],
        features,
        patch_index,
        positive_index,
        bank,
        loss.reshape(owned),
        grad,
        mean_loss,
    )


def solution(mesh):
    in_specs = (P("dp", "bank", None), P("dp", None), P("dp"), P("bank", None))
    out_specs = (P(("dp", "bank")), P(("dp", "bank"), None), P())
    turns = mesh.shape["bank"] // 2
    paired = turns > 1 and turns & (turns - 1) == 0 and mesh.shape["bank"] % 2 == 0
    copies = mesh.shape["dp"]
    paired = paired and copies > 1 and copies & (copies - 1) == 0
    return jax.shard_map(
        on_device if paired else plain, mesh=mesh, in_specs=in_specs, out_specs=out_specs, check_vma=False
    )
```

```python
import functools
import math

import jax
import jax.numpy as jnp
from jax import lax
from jax.experimental import pallas as pl
from jax.experimental.pallas import tpu as pltpu
from jax.sharding import PartitionSpec as P

SOFTMAX_TEMP = 0.07
EPSILON = 1e-05
INV_TEMP = 1.0 / SOFTMAX_TEMP
RATE = INV_TEMP * math.log2(math.e)
STEPS = 32700.0
F32 = jnp.float32
BF16 = jnp.bfloat16
NT = (((1,), (1,)), ((), ()))


def normalize(values):
    scale = lax.rsqrt(jnp.mean(values * values, axis=-1, keepdims=True) + EPSILON)
    return values * scale / math.sqrt(values.shape[-1])


def ring_sum(value, axis):
    size = lax.axis_size(axis)
    pairs = [(i, (i + 1) % size) for i in range(size)]

    def step(_, carry):
        moving, total = carry
        moving = lax.ppermute(moving, axis, pairs)
        return (moving, total + moving)

    return lax.fori_loop(0, size - 1, step, (value, value))[1]


def plain(features, patch_index, positive_index, bank):
    groups = lax.axis_size("bank")
    place = lax.axis_index("bank")
    images, hw_dev, channels = features.shape
    queries_dp = images * patch_index.shape[1]
    owned_rows = queries_dp // groups
    local_pos = patch_index - place * hw_dev
    onehot = (local_pos[:, :, None] == jnp.arange(hw_dev, dtype=jnp.int32)[None, None, :]).astype(BF16)
    picked = jnp.einsum("iph,ihc->ipc", onehot, features, preferred_element_type=F32)
    raw_all = ring_sum(picked.reshape(queries_dp, channels), "bank")
    query_vector = normalize(raw_all).astype(BF16)
    raw_own = lax.dynamic_slice_in_dim(raw_all, place * owned_rows, owned_rows, 0)
    bank_dev = bank.shape[0]
    block_keys = math.gcd(bank_dev, 512)

    def visit(index, carry):
        exponent_sum, weighted = carry
        block = lax.dynamic_slice_in_dim(bank, index * block_keys, block_keys, 0)
        logit = lax.dot_general(query_vector, block, NT, preferred_element_type=F32) / SOFTMAX_TEMP
        terms = jnp.exp(logit - INV_TEMP)
        exponent_sum = exponent_sum + jnp.sum(terms, axis=1)
        weighted = weighted + jnp.dot(terms.astype(BF16), block, preferred_element_type=F32)
        return (exponent_sum, weighted)

    start = (jnp.zeros((queries_dp,), F32), jnp.zeros((queries_dp, channels), F32))
    exponent_sum, weighted = lax.fori_loop(0, bank_dev // block_keys, visit, start)
    key_pos = positive_index - place * bank_dev
    inside = (key_pos >= 0) & (key_pos < bank_dev)
    rows_pos = jnp.clip(key_pos, 0, bank_dev - 1)
    positive_key = bank[rows_pos].astype(F32) * inside[:, None].astype(F32)
    matched = jnp.sum(query_vector.astype(F32) * positive_key, axis=1) / SOFTMAX_TEMP
    own_sum, own_logit, own_weighted, own_positive = (
        lax.dynamic_slice_in_dim(ring_sum(v, "bank"), place * owned_rows, owned_rows, 0)
        for v in (exponent_sum, matched, weighted, positive_key)
    )
    step = (own_weighted / own_sum[:, None] - own_positive) / SOFTMAX_TEMP
    loss = jnp.log(own_sum) + INV_TEMP - own_logit
    _, pullback = jax.vjp(normalize, raw_own)
    query_grad = pullback(step)[0]
    count_all = queries_dp * lax.axis_size("dp")
    mean_loss = ring_sum(ring_sum(jnp.full((8, 128), jnp.sum(loss)), "bank"), "dp")[0, 0] / count_all
    return (loss, query_grad, mean_loss)


def cost(flops):
    return pl.CostEstimate(flops=int(flops), bytes_accessed=1 << 20, transcendentals=0)


def capacity(mean, least, sigmas):
    room = mean + sigmas * math.sqrt(mean)
    return min(least, -(-int(math.ceil(room)) // 16) * 16)


def call(kernel, name, out_shape, flops, room=16, **more):
    params = pltpu.CompilerParams(vmem_limit_bytes=room << 20)
    return pl.pallas_call(
        kernel, out_shape=out_shape, compiler_params=params, cost_estimate=cost(flops), name=name, **more
    )


ANYWHERE = pl.BlockSpec(memory_space=pl.ANY)


def after(value, *others):
    return call(
        lambda *refs: None,
        "after",
        jax.ShapeDtypeStruct(value.shape, value.dtype),
        0,
        in_specs=[ANYWHERE] * (1 + len(others)),
        out_specs=ANYWHERE,
        input_output_aliases={0: 0},
    )(value, *others)


def in_lanes(column_parts, reduce):
    return reduce(column_parts.T, axis=0, keepdims=True)


def ranks_of(code, codes):
    rows, lanes = code.shape
    batch = math.gcd(codes, 16)
    tall = batch * rows
    up = lax.broadcasted_iota(jnp.int32, (lanes, 2 * lanes), 0) <= lax.broadcasted_iota(
        jnp.int32, (lanes, 2 * lanes), 1
    )
    up = up.astype(F32).astype(BF16)
    above = lax.broadcasted_iota(jnp.int32, (tall, tall), 0)
    under = lax.broadcasted_iota(jnp.int32, (tall, tall), 1)
    low = ((above > under) & (above // rows == under // rows)).astype(F32).astype(BF16)
    ranks = jnp.full(code.shape, -1.0, F32)
    most = jnp.zeros((1, lanes), F32)
    for g in range(0, codes, batch):
        mask = jnp.concatenate([(code == g + b).astype(F32) for b in range(batch)], axis=0)
        sums = jnp.dot(mask.astype(BF16), up, preferred_element_type=F32)
        count = sums[:, lanes:]
        rank = sums[:, :lanes] + jnp.dot(low, count.astype(BF16), preferred_element_type=F32)
        rank = rank * mask
        for b in range(batch):
            part = slice(b * rows, (b + 1) * rows)
            ranks = ranks + rank[part]
            most = jnp.maximum(most, jnp.sum(count[part], axis=0, keepdims=True))
    return ranks.astype(jnp.int32), most


def parity_of(shape, owned):
    row = lax.broadcasted_iota(jnp.int32, shape, 0) * shape[1] + lax.broadcasted_iota(jnp.int32, shape, 1)
    return (row // owned) % 2


def by_owner(value, owned):
    rows, lanes = value.shape
    out = []
    for start in range(0, rows * lanes, owned):
        row, lane = divmod(start, lanes)
        if owned <= lanes:
            out.append(value[row : row + 1, lane : lane + owned])
        else:
            out.append(jnp.concatenate([value[row + i : row + i + 1] for i in range(owned // lanes)], axis=1))
    return jnp.concatenate(out, axis=0)


def row_at(ref, place_ref, k):
    return ref[pl.ds(((place_ref[0] // 2) ^ k) * 2 + place_ref[0] % 2, 1), :]


SCALARS = pl.BlockSpec(memory_space=pltpu.SMEM)
NEAR = pl.BlockSpec(memory_space=pltpu.VMEM)


def pick_kernel(
    groups, owned, cap, place_ref, pos_ref, feat_ref, bank_ref, own_ref, other_ref, loc_ref, most_ref, half_ref, sem
):
    half = half_ref.shape[0]
    rows = pl.ds(pl.multiple_of(place_ref[1] * half, half), half)
    fetch = pltpu.make_async_copy(bank_ref.at[rows], half_ref, sem)
    fetch.start()
    place = place_ref[0]
    images, patches = pos_ref.shape
    hw = feat_ref.shape[1]
    pos = pos_ref[...]
    holder = pos // hw
    parity = parity_of(pos.shape, owned)
    ranks, most = ranks_of(holder * 2 + parity, 2 * groups)
    most_ref[...] = jnp.broadcast_to(most, most_ref.shape)
    inner = place % 2
    outer = place // 2
    away = outer ^ (holder // 2)
    side = (holder % 2 + inner) % 2
    stand = jnp.where(away == 1, groups // 2 - 1, jnp.maximum(away - 1, 0))
    loc_ref[...] = by_owner((stand * 2 + side) * cap + ranks, owned)
    local = pos - place * hw
    mine = holder == place
    slot = ranks + jnp.where(parity == inner, 0, cap)
    slot = jnp.where(mine & (ranks < cap), slot, -1)
    total = jnp.zeros((2 * cap, feat_ref.shape[2]), F32)
    where_slot = lax.broadcasted_iota(jnp.int32, (2 * cap, patches), 0)
    where_pos = lax.broadcasted_iota(jnp.int32, (hw, patches), 0)
    for i in range(images):
        chosen = (where_slot == slot[i : i + 1, :]).astype(F32).astype(BF16)
        spots = (where_pos == local[i : i + 1, :]).astype(F32).astype(BF16)
        table = lax.dot_general(chosen, spots, NT, preferred_element_type=F32)
        total = total + jnp.dot(table.astype(BF16), feat_ref[i], preferred_element_type=F32)
    own_ref[...] = total[:cap].astype(BF16)
    other_ref[...] = total[cap:].astype(BF16)
    fetch.wait()


def pick(features, patch_index, bank, place, core, groups, owned, cap):
    images, patches = patch_index.shape
    channels = features.shape[2]
    return call(
        functools.partial(pick_kernel, groups, owned, cap),
        "pick",
        [
            jax.ShapeDtypeStruct((cap, channels), BF16),
            jax.ShapeDtypeStruct((cap, channels), BF16),
            jax.ShapeDtypeStruct((groups, owned), jnp.int32),
            jax.ShapeDtypeStruct((8, patches), F32),
            jax.ShapeDtypeStruct((bank.shape[0] // 2, channels), BF16),
        ],
        3e9,
        in_specs=[
            pl.BlockSpec(memory_space=pltpu.SMEM),
            pl.BlockSpec(memory_space=pltpu.VMEM),
            pl.BlockSpec(memory_space=pltpu.VMEM),
            pl.BlockSpec(memory_space=pl.ANY),
        ],
        scratch_shapes=[pltpu.SemaphoreType.DMA],
    )(jnp.stack([place, core]), patch_index, features, bank)


def keys_kernel(groups, owned, cap, gates, place_ref, index_ref, bank_ref, *refs):
    near_ref, own_ref, other_ref, loc_ref, most_ref, sem = refs[gates:]
    fetch = pltpu.make_async_copy(bank_ref, near_ref, sem)
    fetch.start()
    place = place_ref[0]
    inner = place % 2
    index = index_ref[...]
    keys = near_ref.shape[0]
    holder = index // keys
    parity = parity_of(index.shape, owned)
    ranks, most = ranks_of(holder * 2 + parity, 2 * groups)
    most_ref[...] = jnp.broadcast_to(most, most_ref.shape)
    mine = holder == place
    loc_ref[...] = by_owner(jnp.where(mine, ranks, jnp.where(holder == (place ^ 1), ranks + cap, -1)), owned)
    slot = ranks + jnp.where(parity == inner, 0, cap)
    slot = jnp.where(mine & (ranks < cap), slot, -1)
    local = (index - place * keys + 1).astype(F32)
    rows, lanes = index.shape
    where_slot = lax.broadcasted_iota(jnp.int32, (2 * cap, lanes), 0)
    listed = jnp.zeros((2 * cap, lanes), F32)
    for i in range(rows):
        listed = listed + jnp.where(where_slot == slot[i : i + 1, :], local[i : i + 1, :], 0.0)
    listed = jnp.sum(listed, axis=1, keepdims=True).astype(jnp.int32) - 1
    fetch.wait()
    sub = math.gcd(keys, 256)
    lane = lax.broadcasted_iota(jnp.int32, (2 * cap, sub), 1)
    total = jnp.zeros((2 * cap, near_ref.shape[1]), F32)
    for at in range(0, keys, sub):
        table = (lane + at == listed).astype(F32).astype(BF16)
        total = total + jnp.dot(table, near_ref[at : at + sub, :], preferred_element_type=F32)
    own_ref[...] = total[:cap].astype(BF16)
    other_ref[...] = total[cap:].astype(BF16)


def bring_keys(index, bank, place, groups, owned, cap, gates):
    channels = bank.shape[1]
    return call(
        functools.partial(keys_kernel, groups, owned, cap, len(gates)),
        "keys",
        [
            jax.ShapeDtypeStruct(bank.shape, BF16),
            jax.ShapeDtypeStruct((cap, channels), BF16),
            jax.ShapeDtypeStruct((cap, channels), BF16),
            jax.ShapeDtypeStruct((groups, owned), jnp.int32),
            jax.ShapeDtypeStruct((8, index.shape[1]), F32),
        ],
        2e9,
        in_specs=[pl.BlockSpec(memory_space=pltpu.SMEM), pl.BlockSpec(memory_space=pltpu.VMEM)]
        + [ANYWHERE] * (1 + len(gates)),
        scratch_shapes=[pltpu.SemaphoreType.DMA],
    )(place.reshape(1), index, bank, *gates)


def column_of(row):
    return jnp.broadcast_to(row, (128, row.shape[1])).T[:, 0:1]


def chosen_rows(loc, parts, at):
    column = column_of(loc.astype(F32)).astype(jnp.int32)
    total = jnp.zeros((loc.shape[1], parts[0].shape[1]), F32)
    for ref in parts:
        lane = lax.broadcasted_iota(jnp.int32, (loc.shape[1], ref.shape[0]), 1)
        table = (lane + at == column).astype(F32).astype(BF16)
        total = total + jnp.dot(table, ref[...], preferred_element_type=F32)
        at += ref.shape[0]
    return total


def early_kernel(turns, place_ref, loc_ref, *refs):
    rows = loc_ref.shape[1]
    for k in range(turns):
        chosen = chosen_rows(row_at(loc_ref, place_ref, k), refs[:-1], 0)
        refs[-1][k * rows : (k + 1) * rows, :] = chosen.astype(BF16)


def early(place, loc, parts, turns):
    return call(
        functools.partial(early_kernel, turns),
        "early",
        jax.ShapeDtypeStruct((turns * loc.shape[1], parts[0].shape[1]), BF16),
        2e9,
        in_specs=[SCALARS] + [NEAR] * (1 + len(parts)),
    )(place, loc, *parts)


def arrange_kernel(turns, gates, at, place_ref, loc_ref, early_ref, *refs):
    refs = refs[gates:]
    rows = loc_ref.shape[1]
    parts, (query_ref, raw_ref), blocks = refs[: -2 - turns], refs[-2 - turns : -turns], refs[-turns:]
    for k in range(turns):
        span = slice(k * rows, (k + 1) * rows)
        raw = early_ref[span, :].astype(F32) + chosen_rows(row_at(loc_ref, place_ref, k), parts, at)
        query = normalize(raw).astype(BF16)
        query_ref[span, :] = query
        blocks[k][...] = query
        if k == 0:
            raw_ref[...] = raw.astype(BF16)


def arrange(place, loc, early_rows, parts, at, turns, gates):
    rows, channels = loc.shape[1], parts[0].shape[1]
    out = call(
        functools.partial(arrange_kernel, turns, len(gates), at),
        "arrange",
        [jax.ShapeDtypeStruct((turns * rows, channels), BF16)]
        + [jax.ShapeDtypeStruct((rows, channels), BF16)] * (turns + 1),
        3e9,
        in_specs=[SCALARS] + [NEAR] * 2 + [ANYWHERE] * len(gates) + [NEAR] * len(parts),
    )(place, loc, early_rows, *gates, *parts)
    return out[0], out[1], out[2:]


def sweep(query, keys, total, pushed):
    sub = math.gcd(keys.shape[0], 1024)
    for at in range(0, keys.shape[0], sub):
        block = keys[at : at + sub, :]
        logit = lax.dot_general(query, block, NT, preferred_element_type=F32)
        terms = jnp.exp2(logit * RATE - RATE)
        if total is not None:
            for c in range(0, sub, 128):
                total = total + terms[:, c : c + 128]
        pushed = pushed + jnp.dot(terms.astype(BF16), block, preferred_element_type=F32)
    return total, pushed


def first_kernel(turns, gates, query_ref, keys_ref, *refs):
    total_ref, blocks = refs[gates], refs[gates + 1 :]
    rows = query_ref.shape[0] // turns
    for k in range(turns):
        part = slice(k * rows, (k + 1) * rows)
        total_ref[part, :], blocks[k][...] = sweep(
            query_ref[part, :], keys_ref, jnp.zeros((rows, 128), F32), jnp.zeros(blocks[k].shape, F32)
        )


def first(query, keys, turns, gates):
    rows, channels = query.shape
    out = call(
        functools.partial(first_kernel, turns, len(gates)),
        "first",
        [jax.ShapeDtypeStruct((rows, 128), F32)] + [jax.ShapeDtypeStruct((rows // turns, channels), F32)] * turns,
        8 * rows * keys.shape[0] * channels,
        room=24,
        in_specs=[pl.BlockSpec(memory_space=pltpu.VMEM)] * 2 + [ANYWHERE] * len(gates),
    )(query, keys, *gates)
    return out[0], out[1:]


def lane_sums(query, keys, total):
    sub = math.gcd(keys.shape[0], 256)
    for at in range(0, keys.shape[0], sub):
        logit = lax.dot_general(query, keys[at : at + sub, :], NT, preferred_element_type=F32)
        terms = jnp.exp2(logit * RATE - RATE)
        for c in range(0, sub, 128):
            total = total + terms[:, c : c + 128]
    return total


def far_kernel(count, turns, query_ref, total_in, *refs):
    note_ref = refs[count]
    rows = note_ref.shape[1]
    total = total_in[...]
    for ref in refs[:count]:
        total = lane_sums(query_ref[...], ref, total)
    note_ref[...] = jnp.zeros(note_ref.shape, F32)
    for t in range(turns):
        note_ref[t : t + 1, :] = in_lanes(total[t * rows : (t + 1) * rows], jnp.sum)


def far_totals(query, total, keys, turns):
    lines = -(-2 * turns // 8) * 8
    return call(
        functools.partial(far_kernel, len(keys), turns),
        "far",
        jax.ShapeDtypeStruct((lines, query.shape[0] // turns), F32),
        2 * query.shape[0] * sum(k.shape[0] for k in keys) * query.shape[1],
        room=24,
    )(query, total, *keys)


def spread_kernel(turns, place_ref, note_in, loc_ref, own_ref, side_ref, *refs):
    blocks, note_ref, outs = refs[:turns], refs[turns], refs[turns + 1 :]
    note_ref[...] = note_in[...]
    for t in range(turns):
        positive = chosen_rows(row_at(loc_ref, place_ref, t), [own_ref, side_ref], 0)
        outs[t][...] = positive.astype(BF16)
        matched = in_lanes(blocks[t][...].astype(F32) * positive, jnp.sum)
        note_ref[turns + t : turns + t + 1, :] = matched / SOFTMAX_TEMP


def spread(place, note, loc, own, side, blocks):
    turns = len(blocks)
    rows, channels = blocks[0].shape
    out = call(
        functools.partial(spread_kernel, turns),
        "spread",
        [jax.ShapeDtypeStruct(note.shape, F32)] + [jax.ShapeDtypeStruct((rows, channels), BF16)] * turns,
        1e9,
        in_specs=[SCALARS] + [NEAR] * (4 + turns),
    )(place, note, loc, own, side, *blocks)
    return out[0], out[1:]


def exponent(size):
    return jnp.ceil(jnp.log2(jnp.maximum(size, 1e-30)))


def last_kernel(query_ref, pushed_in, gate_ref, *refs):
    pushed = pushed_in[...]
    for ref in refs[:-1]:
        _, pushed = sweep(query_ref[...], ref, None, pushed)
    refs[-1][...] = pushed


def last(query, pushed, keys, gate):
    rows, channels = query.shape
    return call(
        last_kernel,
        "last",
        jax.ShapeDtypeStruct((rows, channels), F32),
        4 * rows * sum(v.shape[0] for v in keys) * channels,
        in_specs=[pl.BlockSpec(memory_space=pltpu.VMEM)] * 2 + [ANYWHERE] + [pl.BlockSpec(memory_space=pltpu.VMEM)] * len(keys),
    )(query, pushed, gate, *keys)


def step_of(k, pushed_ref, positive_ref, totals_ref):
    return pushed_ref[...] / column_of(totals_ref[k : k + 1, :]) - positive_ref[...].astype(F32)


def code_kernel(k, pushed_ref, positive_ref, totals_ref, gate_ref, sent_ref):
    step = step_of(k, pushed_ref, positive_ref, totals_ref)
    size = jnp.abs(step)
    wide = size[:, :128]
    for c in range(128, size.shape[1], 128):
        wide = jnp.maximum(wide, size[:, c : c + 128])
    rows = step.shape[0]
    scale = jnp.exp2(-exponent(jnp.max(wide, axis=1, keepdims=True))) * STEPS
    sent_ref[:rows, :] = jnp.round(step * scale).astype(jnp.int32).astype(jnp.int16)
    power = exponent(in_lanes(wide, jnp.max)).astype(jnp.int32)
    rest = sent_ref.shape[1] - rows
    if rest:
        power = jnp.concatenate([power, jnp.zeros((1, rest), jnp.int32)], axis=1)
    sent_ref[rows:, :] = jnp.broadcast_to(power, (sent_ref.shape[0] - rows, sent_ref.shape[1])).astype(jnp.int16)


def code(pushed, positive, totals, k, gate):
    rows, channels = pushed.shape
    shape = jax.ShapeDtypeStruct((rows + 16, channels), jnp.int16)
    return call(
        functools.partial(code_kernel, k),
        "code",
        shape,
        2e8,
        in_specs=[pl.BlockSpec(memory_space=pltpu.VMEM)] * 3 + [ANYWHERE],
    )(pushed, positive, totals, gate)


def settle_kernel(turns, caps, note_ref, most_ref, held_ref, *refs):
    came = refs[: turns - 1]
    loss_ref, totals_ref, word_ref = refs[turns - 1 :]
    line = jnp.zeros(loss_ref.shape, F32)
    for t in range(turns):
        total = note_ref[t : t + 1, :]
        matched = note_ref[turns + t : turns + t + 1, :]
        for k in range(1, turns):
            ref = came[k - 1]
            total = total + ref[t ^ k : (t ^ k) + 1, :]
            matched = matched + ref[turns + (t ^ k) : turns + (t ^ k) + 1, :]
        totals_ref[t : t + 1, :] = total
        loss = jnp.log(total) + INV_TEMP - matched
        if t == 0:
            loss_ref[...] = loss
        line = line + loss
    over = (jnp.max(most_ref[...]) > caps[0]) | (jnp.max(held_ref[...]) > caps[1])
    word_ref[...] = jnp.zeros(word_ref.shape, F32)
    word_ref[0:1, 0:1] = jnp.sum(line, axis=1, keepdims=True)
    word_ref[1:2, :] = jnp.full((1, word_ref.shape[1]), jnp.where(over, 1.0, 0.0))


def settle(note, most, held, came, turns, caps):
    rows = note.shape[1]
    return call(
        functools.partial(settle_kernel, turns, caps),
        "settle",
        [
            jax.ShapeDtypeStruct((1, rows), F32),
            jax.ShapeDtypeStruct((-(-turns // 8) * 8, rows), F32),
            jax.ShapeDtypeStruct((8, 128), F32),
        ],
        1e8,
    )(note, most, held, *came)


def finish_kernel(count, queries, raw_ref, positive_ref, own_ref, totals_ref, loss_in, word_ref, came_ref, *refs):
    out_ref, loss_ref, mean_ref, flag_ref, grad_ref, sems = refs[count:]
    loss_store = pltpu.make_async_copy(loss_in, loss_ref, sems.at[0])
    loss_store.start()
    word = word_ref[...] + came_ref[...]
    mean_ref[0, 0] = jnp.sum(word[0:1, :]) * (1.0 / queries)
    flag_ref[0, 0] = (jnp.max(word[1:2, :]) > 0.5).astype(jnp.int32)
    rows = raw_ref.shape[0]
    scales = [ref[rows : rows + 16, :rows].astype(jnp.int32).astype(F32)[0:1, :] for ref in refs[:count]]
    scales = [jnp.exp2(v) * (1.0 / STEPS) for v in scales]
    fill = -count % 128
    turned = jnp.concatenate(scales + [jnp.zeros((fill, rows), F32)], axis=0).T
    step = step_of(0, own_ref, positive_ref, totals_ref)
    for j in range(count):
        step = step + refs[j][:rows, :].astype(jnp.int32).astype(F32) * turned[:, j : j + 1]
    step = step * INV_TEMP
    raw = raw_ref[...].astype(F32)
    scale = lax.rsqrt(jnp.mean(raw * raw, axis=-1, keepdims=True) + EPSILON)
    inner = jnp.mean(step * raw, axis=-1, keepdims=True)
    grad_ref[...] = (step - raw * (scale * scale * inner)) * (scale / math.sqrt(raw.shape[1]))
    store = pltpu.make_async_copy(grad_ref, out_ref, sems.at[1])
    store.start()
    loss_store.wait()
    store.wait()


def finish(raw, positive, own, totals, loss, word, came, parts, queries):
    return call(
        functools.partial(finish_kernel, len(parts), queries),
        "finish",
        [
            jax.ShapeDtypeStruct(own.shape, F32),
            jax.ShapeDtypeStruct(loss.shape, F32),
            jax.ShapeDtypeStruct((1, 1), F32),
            jax.ShapeDtypeStruct((1, 1), jnp.int32),
        ],
        5e8,
        in_specs=[NEAR] * (7 + len(parts)),
        out_specs=[pl.BlockSpec(memory_space=pltpu.HBM)] * 2 + [SCALARS] * 2,
        scratch_shapes=[pltpu.VMEM(own.shape, F32), pltpu.SemaphoreType.DMA((2,))],
    )(raw, positive, own, totals, loss, word, came, *parts)


def on_device(features, patch_index, positive_index, bank):
    groups, copies = lax.axis_size("bank"), lax.axis_size("dp")
    place = lax.axis_index("bank")
    core = lax.axis_index("dp") % 2
    images, hw_dev, channels = features.shape
    queries_dp = images * patch_index.shape[1]
    owned = queries_dp // groups
    turns = groups // 2
    inner, outer = place % 2, place // 2
    bank_dev = bank.shape[0]
    across = [(b, b ^ 1) for b in range(groups)]
    swap = [(c, c ^ 1) for c in range(copies)]

    def turn(value, k):
        pairs = [(b, b ^ (2 * k)) for b in range(groups)]
        return lax.ppermute(value, "bank", pairs)

    def to_all(values):
        return [values[0]] + [turn(values[k], k) for k in [*range(2, turns), 1]]

    cap = capacity(queries_dp / groups / 2, queries_dp // 2, 4.0)
    own_set, other_set, loc, most, half = pick(features, patch_index, bank, place, core, groups, owned, cap)
    from_side = lax.ppermute(other_set, "bank", across)
    fetched = lax.ppermute(half, "bank", across)
    held_rows = jnp.concatenate([own_set, from_side])
    parts = to_all([held_rows] * turns)

    cap_pos = capacity(queries_dp / groups / 2, queries_dp // 2, 5.0)
    index = positive_index.reshape(images, -1)
    near_keys, own_keys, other_keys, key_loc, held = bring_keys(
        index, bank, place, groups, owned, cap_pos, [from_side]
    )
    side_keys = lax.ppermute(other_keys, "bank", across)

    here = place.reshape(1)
    early_rows = early(here, loc, parts[:2], turns)
    query, raw, blocks = arrange(here, loc, early_rows, parts[2:], 4 * cap, turns, [near_keys, key_loc])

    total, pushed = first(query, near_keys, turns, [])
    fetched = after(fetched, total)
    far_keys = [fetched, lax.ppermute(fetched, "dp", swap)]
    far_note = far_totals(query, total, far_keys, turns)
    note, positive = spread(here, far_note, key_loc, own_keys, side_keys, blocks)
    came = to_all([note] * turns)
    came = [came[-1], *came[1:-1]]
    loss, totals, word = settle(note, most, held, came, turns, (cap, cap_pos))
    moved = [None] * turns
    order = [*range(2, turns)]
    order.insert(1, 1)
    whole = {k: last(blocks[k], pushed[k], far_keys, note) for k in order[:3]}
    gate = totals
    for k in order:
        if k not in whole:
            whole[k] = last(blocks[k], pushed[k], far_keys, gate)
        sent = code(whole[k], positive[k], totals, k, gate)
        moved[k] = turn(sent, k)
        gate = sent
    for axis, step in [("dp", 1), ("bank", 1)] + [("dp", 1 << i) for i in range(1, copies.bit_length() - 1)]:
        pairs = [(i, i ^ step) for i in range(lax.axis_size(axis))]
        last_word, came_word = word, lax.ppermute(word, axis, pairs)
        word = last_word + came_word
        if step == 1 and axis == "dp":
            own = last(blocks[0], pushed[0], far_keys, word)
    grad, loss, mean_loss, flag = finish(
        raw, positive[0], own, totals, loss, last_word, came_word, moved[1:], queries_dp * copies
    )
    return lax.cond(
        flag.reshape(()) > 0,
        lambda *a: plain(*a[:4]),
        lambda *a: a[4:],
        features,
        patch_index,
        positive_index,
        bank,
        loss.reshape(owned),
        grad,
        mean_loss.reshape(()),
    )


def solution(mesh):
    in_specs = (P("dp", "bank", None), P("dp", None), P("dp"), P("bank", None))
    out_specs = (P(("dp", "bank")), P(("dp", "bank"), None), P())
    turns = mesh.shape["bank"] // 2
    paired = turns > 1 and turns & (turns - 1) == 0 and mesh.shape["bank"] % 2 == 0
    copies = mesh.shape["dp"]
    paired = paired and copies > 1 and copies & (copies - 1) == 0
    return jax.shard_map(
        on_device if paired else plain, mesh=mesh, in_specs=in_specs, out_specs=out_specs, check_vma=False
    )
```

```python
import functools
import math

import jax
import jax.numpy as jnp
from jax import lax
from jax.experimental import pallas as pl
from jax.experimental.pallas import tpu as pltpu
from jax.sharding import PartitionSpec as P

SOFTMAX_TEMP = 0.07
EPSILON = 1e-05
INV_TEMP = 1.0 / SOFTMAX_TEMP
RATE = INV_TEMP * math.log2(math.e)
STEPS = 32700.0
F32 = jnp.float32
BF16 = jnp.bfloat16
NT = (((1,), (1,)), ((), ()))


def normalize(values):
    scale = lax.rsqrt(jnp.mean(values * values, axis=-1, keepdims=True) + EPSILON)
    return values * scale / math.sqrt(values.shape[-1])


def ring_sum(value, axis):
    size = lax.axis_size(axis)
    pairs = [(i, (i + 1) % size) for i in range(size)]

    def step(_, carry):
        moving, total = carry
        moving = lax.ppermute(moving, axis, pairs)
        return (moving, total + moving)

    return lax.fori_loop(0, size - 1, step, (value, value))[1]


def plain(features, patch_index, positive_index, bank):
    groups = lax.axis_size("bank")
    place = lax.axis_index("bank")
    images, hw_dev, channels = features.shape
    queries_dp = images * patch_index.shape[1]
    owned_rows = queries_dp // groups
    local_pos = patch_index - place * hw_dev
    onehot = (local_pos[:, :, None] == jnp.arange(hw_dev, dtype=jnp.int32)[None, None, :]).astype(BF16)
    picked = jnp.einsum("iph,ihc->ipc", onehot, features, preferred_element_type=F32)
    raw_all = ring_sum(picked.reshape(queries_dp, channels), "bank")
    query_vector = normalize(raw_all).astype(BF16)
    raw_own = lax.dynamic_slice_in_dim(raw_all, place * owned_rows, owned_rows, 0)
    bank_dev = bank.shape[0]
    block_keys = math.gcd(bank_dev, 512)

    def visit(index, carry):
        exponent_sum, weighted = carry
        block = lax.dynamic_slice_in_dim(bank, index * block_keys, block_keys, 0)
        logit = lax.dot_general(query_vector, block, NT, preferred_element_type=F32) / SOFTMAX_TEMP
        terms = jnp.exp(logit - INV_TEMP)
        exponent_sum = exponent_sum + jnp.sum(terms, axis=1)
        weighted = weighted + jnp.dot(terms.astype(BF16), block, preferred_element_type=F32)
        return (exponent_sum, weighted)

    start = (jnp.zeros((queries_dp,), F32), jnp.zeros((queries_dp, channels), F32))
    exponent_sum, weighted = lax.fori_loop(0, bank_dev // block_keys, visit, start)
    key_pos = positive_index - place * bank_dev
    inside = (key_pos >= 0) & (key_pos < bank_dev)
    rows_pos = jnp.clip(key_pos, 0, bank_dev - 1)
    positive_key = bank[rows_pos].astype(F32) * inside[:, None].astype(F32)
    matched = jnp.sum(query_vector.astype(F32) * positive_key, axis=1) / SOFTMAX_TEMP
    own_sum, own_logit, own_weighted, own_positive = (
        lax.dynamic_slice_in_dim(ring_sum(v, "bank"), place * owned_rows, owned_rows, 0)
        for v in (exponent_sum, matched, weighted, positive_key)
    )
    step = (own_weighted / own_sum[:, None] - own_positive) / SOFTMAX_TEMP
    loss = jnp.log(own_sum) + INV_TEMP - own_logit
    _, pullback = jax.vjp(normalize, raw_own)
    query_grad = pullback(step)[0]
    count_all = queries_dp * lax.axis_size("dp")
    mean_loss = ring_sum(ring_sum(jnp.full((8, 128), jnp.sum(loss)), "bank"), "dp")[0, 0] / count_all
    return (loss, query_grad, mean_loss)


def cost(flops):
    return pl.CostEstimate(flops=int(flops), bytes_accessed=1 << 20, transcendentals=0)


def capacity(mean, least, sigmas):
    room = mean + sigmas * math.sqrt(mean)
    return min(least, -(-int(math.ceil(room)) // 16) * 16)


def call(kernel, name, out_shape, flops, room=16, **more):
    params = pltpu.CompilerParams(vmem_limit_bytes=room << 20)
    return pl.pallas_call(
        kernel, out_shape=out_shape, compiler_params=params, cost_estimate=cost(flops), name=name, **more
    )


ANYWHERE = pl.BlockSpec(memory_space=pl.ANY)


def after(value, *others):
    return call(
        lambda *refs: None,
        "after",
        jax.ShapeDtypeStruct(value.shape, value.dtype),
        0,
        in_specs=[ANYWHERE] * (1 + len(others)),
        out_specs=ANYWHERE,
        input_output_aliases={0: 0},
    )(value, *others)


def in_lanes(column_parts, reduce):
    return reduce(column_parts.T, axis=0, keepdims=True)


def ranks_of(code, codes):
    rows, lanes = code.shape
    batch = math.gcd(codes, 16)
    tall = batch * rows
    up = lax.broadcasted_iota(jnp.int32, (lanes, 2 * lanes), 0) <= lax.broadcasted_iota(
        jnp.int32, (lanes, 2 * lanes), 1
    )
    up = up.astype(F32).astype(BF16)
    above = lax.broadcasted_iota(jnp.int32, (tall, tall), 0)
    under = lax.broadcasted_iota(jnp.int32, (tall, tall), 1)
    low = ((above > under) & (above // rows == under // rows)).astype(F32).astype(BF16)
    ranks = jnp.full(code.shape, -1.0, F32)
    most = jnp.zeros((1, lanes), F32)
    for g in range(0, codes, batch):
        mask = jnp.concatenate([(code == g + b).astype(F32) for b in range(batch)], axis=0)
        sums = jnp.dot(mask.astype(BF16), up, preferred_element_type=F32)
        count = sums[:, lanes:]
        rank = sums[:, :lanes] + jnp.dot(low, count.astype(BF16), preferred_element_type=F32)
        rank = rank * mask
        for b in range(batch):
            part = slice(b * rows, (b + 1) * rows)
            ranks = ranks + rank[part]
            most = jnp.maximum(most, jnp.sum(count[part], axis=0, keepdims=True))
    return ranks.astype(jnp.int32), most


def parity_of(shape, owned):
    row = lax.broadcasted_iota(jnp.int32, shape, 0) * shape[1] + lax.broadcasted_iota(jnp.int32, shape, 1)
    return (row // owned) % 2


def by_owner(value, owned):
    rows, lanes = value.shape
    out = []
    for start in range(0, rows * lanes, owned):
        row, lane = divmod(start, lanes)
        if owned <= lanes:
            out.append(value[row : row + 1, lane : lane + owned])
        else:
            out.append(jnp.concatenate([value[row + i : row + i + 1] for i in range(owned // lanes)], axis=1))
    return jnp.concatenate(out, axis=0)


def row_at(ref, place_ref, k):
    return ref[pl.ds(((place_ref[0] // 2) ^ k) * 2 + place_ref[0] % 2, 1), :]


SCALARS = pl.BlockSpec(memory_space=pltpu.SMEM)
NEAR = pl.BlockSpec(memory_space=pltpu.VMEM)


def pick_kernel(
    owned, cap, place_ref, pos_ref, feat_ref, bank_ref, own_ref, other_ref, relay_ref, rest_ref, table, sems
):
    fetches = []
    for i, (ref, at) in enumerate([(relay_ref, place_ref[1]), (rest_ref, place_ref[2])]):
        span = pl.ds(pl.multiple_of(at * 16, 16), ref.shape[0])
        fetches.append(pltpu.make_async_copy(bank_ref.at[span], ref, sems.at[i]))
        fetches[-1].start()
    place = place_ref[0]
    images, patches = pos_ref.shape
    hw = feat_ref.shape[1]
    pos = pos_ref[...]
    mine = pos // hw == place
    parity = (parity_of(pos.shape, owned) + place) % 2
    code = jnp.where(mine, parity, 2)
    ranks, _ = ranks_of(code, 2)
    slot = ranks + parity * cap
    slot = jnp.where(mine & (ranks < cap), slot, -1)
    local = jnp.where(mine, pos - place * hw, -1)
    batch = math.gcd(images, max(1, 256 // patches))
    where_slot = lax.broadcasted_iota(jnp.int32, (2 * cap, batch * patches), 0)
    where_pos = lax.broadcasted_iota(jnp.int32, (batch * hw, batch * patches), 0)
    for i in range(0, images, batch):
        slots = jnp.concatenate([slot[i + b : i + b + 1, :] for b in range(batch)], axis=1)
        locals_ = jnp.concatenate(
            [jnp.where(local[i + b : i + b + 1, :] < 0, -1, local[i + b : i + b + 1, :] + b * hw) for b in range(batch)],
            axis=1,
        )
        chosen = (where_slot == slots).astype(F32).astype(BF16)
        spots = (where_pos == locals_).astype(F32).astype(BF16)
        part = lax.dot_general(chosen, spots, NT, preferred_element_type=F32)
        table[:, i * hw : (i + batch) * hw] = part.astype(BF16)
    rows = feat_ref[...].reshape(images * hw, feat_ref.shape[2])
    total = jnp.dot(table[...], rows, preferred_element_type=F32)
    own_ref[...] = total[:cap].astype(BF16)
    other_ref[...] = total[cap:].astype(BF16)
    for fetch in fetches:
        fetch.wait()


def pick(features, patch_index, bank, numbers, relay, rest, owned, cap):
    images, hw, channels = features.shape
    return call(
        functools.partial(pick_kernel, owned, cap),
        "pick",
        [
            jax.ShapeDtypeStruct((cap, channels), BF16),
            jax.ShapeDtypeStruct((cap, channels), BF16),
            jax.ShapeDtypeStruct((relay, channels), BF16),
            jax.ShapeDtypeStruct((rest, channels), BF16),
        ],
        3e9,
        in_specs=[SCALARS, NEAR, NEAR, ANYWHERE],
        scratch_shapes=[pltpu.VMEM((2 * cap, images * hw), BF16), pltpu.SemaphoreType.DMA((2,))],
    )(numbers, patch_index, features, bank)


def locate_kernel(groups, owned, cap, hw, gates, place_ref, pos_ref, *refs):
    loc_ref, most_ref = refs[gates:]
    place = place_ref[0]
    pos = pos_ref[...]
    holder = pos // hw
    ranks, most = ranks_of(holder * 2 + parity_of(pos.shape, owned), 2 * groups)
    most_ref[...] = jnp.broadcast_to(most, most_ref.shape)
    away = (place // 2) ^ (holder // 2)
    side = (holder % 2 + place) % 2
    stand = jnp.where(away == 1, groups // 2 - 1, jnp.maximum(away - 1, 0))
    loc_ref[...] = by_owner((stand * 2 + side) * cap + ranks, owned)


def locate(patch_index, place, groups, owned, cap, hw, gates):
    return call(
        functools.partial(locate_kernel, groups, owned, cap, hw, len(gates)),
        "locate",
        [
            jax.ShapeDtypeStruct((groups, owned), jnp.int32),
            jax.ShapeDtypeStruct((8, patch_index.shape[1]), F32),
        ],
        1e9,
        in_specs=[SCALARS, NEAR] + [ANYWHERE] * len(gates),
    )(place.reshape(1), patch_index, *gates)


def keys_kernel(groups, owned, cap, relay, gates, place_ref, index_ref, bank_ref, *refs):
    near_ref, own_ref, list_ref, loc_ref, most_ref, sem = refs[gates:]
    fetch = pltpu.make_async_copy(bank_ref, near_ref, sem)
    fetch.start()
    place, core, line = place_ref[0], place_ref[1], place_ref[2]
    index = index_ref[...]
    keys = near_ref.shape[0]
    holder = index // keys
    parity = parity_of(index.shape, owned)
    ranks, most = ranks_of(holder * 2 + parity, 2 * groups)
    most_ref[...] = jnp.broadcast_to(most, most_ref.shape)
    mine, theirs = holder == place, holder == (place ^ 1)
    loc_ref[...] = by_owner(jnp.where(mine, ranks, jnp.where(theirs, ranks + cap, -1)), owned)
    slot = jnp.where(theirs, ranks + cap, ranks)
    slot = jnp.where((mine | theirs) & (ranks < cap) & (parity == place % 2), slot, -1)
    half = keys // 2
    rest = half - 2 * relay
    far = index - (place ^ 1) * keys
    other = jnp.where(far // half == core, 0, 1)
    offset = far % half
    strip = jnp.where(offset // relay == line, 0, 1)
    far = jnp.where(
        offset < 2 * relay,
        (strip * 2 + other) * relay + offset % relay,
        4 * relay + other * rest + offset - 2 * relay,
    )
    local = (jnp.where(mine, index - place * keys, far) + 1).astype(F32)
    rows, lanes = index.shape
    where_slot = lax.broadcasted_iota(jnp.int32, (2 * cap, lanes), 0)
    listed = jnp.zeros((2 * cap, lanes), F32)
    for i in range(rows):
        listed = listed + jnp.where(where_slot == slot[i : i + 1, :], local[i : i + 1, :], 0.0)
    listed = jnp.sum(listed, axis=1, keepdims=True).astype(jnp.int32) - 1
    list_ref[...] = listed[cap:]
    fetch.wait()
    own_ref[...] = listed_rows(listed[:cap], [near_ref]).astype(BF16)


def listed_rows(listed, parts):
    total = jnp.zeros((listed.shape[0], parts[0].shape[1]), F32)
    start = 0
    for ref in parts:
        sub = math.gcd(ref.shape[0], 256)
        lane = lax.broadcasted_iota(jnp.int32, (listed.shape[0], sub), 1)
        for at in range(0, ref.shape[0], sub):
            table = (lane + (start + at) == listed).astype(F32).astype(BF16)
            total = total + jnp.dot(table, ref[at : at + sub, :], preferred_element_type=F32)
        start += ref.shape[0]
    return total


def bring_keys(index, bank, numbers, groups, owned, cap, relay, gates):
    channels = bank.shape[1]
    return call(
        functools.partial(keys_kernel, groups, owned, cap, relay, len(gates)),
        "keys",
        [
            jax.ShapeDtypeStruct(bank.shape, BF16),
            jax.ShapeDtypeStruct((cap, channels), BF16),
            jax.ShapeDtypeStruct((cap, 1), jnp.int32),
            jax.ShapeDtypeStruct((groups, owned), jnp.int32),
            jax.ShapeDtypeStruct((8, index.shape[1]), F32),
        ],
        2e9,
        in_specs=[SCALARS, NEAR] + [ANYWHERE] * (1 + len(gates)),
        scratch_shapes=[pltpu.SemaphoreType.DMA],
    )(numbers, index, bank, *gates)


def column_of(row):
    return jnp.broadcast_to(row, (128, row.shape[1])).T[:, 0:1]


def chosen_rows(loc, parts, at):
    column = column_of(loc.astype(F32)).astype(jnp.int32)
    total = jnp.zeros((loc.shape[1], parts[0].shape[1]), F32)
    for ref in parts:
        lane = lax.broadcasted_iota(jnp.int32, (loc.shape[1], ref.shape[0]), 1)
        table = (lane + at == column).astype(F32).astype(BF16)
        total = total + jnp.dot(table, ref[...], preferred_element_type=F32)
        at += ref.shape[0]
    return total


def early_kernel(turns, gates, place_ref, loc_ref, *refs):
    refs = refs[gates:]
    rows = loc_ref.shape[1]
    for k in range(turns):
        chosen = chosen_rows(row_at(loc_ref, place_ref, k), refs[:-1], 0)
        refs[-1][k * rows : (k + 1) * rows, :] = chosen.astype(BF16)


def early(place, loc, parts, turns, gates):
    return call(
        functools.partial(early_kernel, turns, len(gates)),
        "early",
        jax.ShapeDtypeStruct((turns * loc.shape[1], parts[0].shape[1]), BF16),
        2e9,
        in_specs=[SCALARS, NEAR] + [ANYWHERE] * len(gates) + [NEAR] * len(parts),
    )(place, loc, *gates, *parts)


def arrange_kernel(turns, gates, at, place_ref, loc_ref, early_ref, *refs):
    refs = refs[gates:]
    rows = loc_ref.shape[1]
    parts, (query_ref, raw_ref), blocks = refs[: -2 - turns], refs[-2 - turns : -turns], refs[-turns:]
    for k in range(turns):
        span = slice(k * rows, (k + 1) * rows)
        raw = early_ref[span, :].astype(F32) + chosen_rows(row_at(loc_ref, place_ref, k), parts, at)
        query = normalize(raw).astype(BF16)
        query_ref[span, :] = query
        blocks[k][...] = query
        if k == 0:
            raw_ref[...] = raw.astype(BF16)


def arrange(place, loc, early_rows, parts, at, turns, gates):
    rows, channels = loc.shape[1], parts[0].shape[1]
    out = call(
        functools.partial(arrange_kernel, turns, len(gates), at),
        "arrange",
        [jax.ShapeDtypeStruct((turns * rows, channels), BF16)]
        + [jax.ShapeDtypeStruct((rows, channels), BF16)] * (turns + 1),
        3e9,
        in_specs=[SCALARS] + [NEAR] * 2 + [ANYWHERE] * len(gates) + [NEAR] * len(parts),
    )(place, loc, early_rows, *gates, *parts)
    return out[0], out[1], out[2:]


def sweep(query, keys, total, pushed):
    sub = math.gcd(keys.shape[0], 1024)
    for at in range(0, keys.shape[0], sub):
        block = keys[at : at + sub, :]
        logit = lax.dot_general(query, block, NT, preferred_element_type=F32)
        terms = jnp.exp2(logit * RATE - RATE)
        if total is not None:
            for c in range(0, sub, 128):
                total = total + terms[:, c : c + 128]
        pushed = pushed + jnp.dot(terms.astype(BF16), block, preferred_element_type=F32)
    return total, pushed


def first_kernel(turns, gates, query_ref, keys_ref, *refs):
    total_ref, blocks = refs[gates], refs[gates + 1 :]
    rows = query_ref.shape[0] // turns
    for k in range(turns):
        part = slice(k * rows, (k + 1) * rows)
        total_ref[part, :], blocks[k][...] = sweep(
            query_ref[part, :], keys_ref, jnp.zeros((rows, 128), F32), jnp.zeros(blocks[k].shape, F32)
        )


def first(query, keys, turns, gates):
    rows, channels = query.shape
    out = call(
        functools.partial(first_kernel, turns, len(gates)),
        "first",
        [jax.ShapeDtypeStruct((rows, 128), F32)] + [jax.ShapeDtypeStruct((rows // turns, channels), F32)] * turns,
        8 * rows * keys.shape[0] * channels,
        room=24,
        in_specs=[pl.BlockSpec(memory_space=pltpu.VMEM)] * 2 + [ANYWHERE] * len(gates),
    )(query, keys, *gates)
    return out[0], out[1:]


def lane_sums(query, keys, total):
    sub = math.gcd(keys.shape[0], 256)
    for at in range(0, keys.shape[0], sub):
        logit = lax.dot_general(query, keys[at : at + sub, :], NT, preferred_element_type=F32)
        terms = jnp.exp2(logit * RATE - RATE)
        for c in range(0, sub, 128):
            total = total + terms[:, c : c + 128]
    return total


def far_kernel(count, turns, place_ref, loc_ref, query_ref, total_in, own_ref, list_ref, *refs):
    keys, note_ref, outs, side_ref = refs[:count], refs[count], refs[count + 1 : -1], refs[-1]
    rows = note_ref.shape[1]
    side_ref[...] = listed_rows(list_ref[...], keys).astype(BF16)
    total = total_in[...]
    for ref in keys:
        total = lane_sums(query_ref[...], ref, total)
    note_ref[...] = jnp.zeros(note_ref.shape, F32)
    for t in range(turns):
        part = slice(t * rows, (t + 1) * rows)
        note_ref[t : t + 1, :] = in_lanes(total[part], jnp.sum)
        positive = chosen_rows(row_at(loc_ref, place_ref, t), [own_ref, side_ref], 0)
        outs[t][...] = positive.astype(BF16)
        matched = in_lanes(query_ref[part, :].astype(F32) * positive, jnp.sum)
        note_ref[turns + t : turns + t + 1, :] = matched / SOFTMAX_TEMP


def far_totals(place, loc, query, total, own, listed, keys, turns):
    lines = -(-2 * turns // 8) * 8
    rows, channels = query.shape[0] // turns, query.shape[1]
    out = call(
        functools.partial(far_kernel, len(keys), turns),
        "far",
        [jax.ShapeDtypeStruct((lines, rows), F32)] + [jax.ShapeDtypeStruct((rows, channels), BF16)] * turns,
        2 * query.shape[0] * sum(k.shape[0] for k in keys) * channels,
        room=24,
        in_specs=[SCALARS] + [NEAR] * (5 + len(keys)),
        scratch_shapes=[pltpu.VMEM(own.shape, BF16)],
    )(place, loc, query, total, own, listed, *keys)
    return out[0], out[1:]


def exponent(size):
    return jnp.ceil(jnp.log2(jnp.maximum(size, 1e-30)))


def last_kernel(query_ref, pushed_in, gate_ref, *refs):
    pushed = pushed_in[...]
    for ref in refs[:-1]:
        _, pushed = sweep(query_ref[...], ref, None, pushed)
    refs[-1][...] = pushed


def last(query, pushed, keys, gate):
    rows, channels = query.shape
    return call(
        last_kernel,
        "last",
        jax.ShapeDtypeStruct((rows, channels), F32),
        4 * rows * sum(v.shape[0] for v in keys) * channels,
        in_specs=[pl.BlockSpec(memory_space=pltpu.VMEM)] * 2 + [ANYWHERE] + [pl.BlockSpec(memory_space=pltpu.VMEM)] * len(keys),
    )(query, pushed, gate, *keys)


def step_of(k, pushed_ref, positive_ref, totals_ref):
    return pushed_ref[...] / column_of(totals_ref[k : k + 1, :]) - positive_ref[...].astype(F32)


def code_kernel(k, pushed_ref, positive_ref, totals_ref, *refs):
    sent_ref = refs[-1]
    step = step_of(k, pushed_ref, positive_ref, totals_ref)
    size = jnp.abs(step)
    wide = size[:, :128]
    for c in range(128, size.shape[1], 128):
        wide = jnp.maximum(wide, size[:, c : c + 128])
    rows = step.shape[0]
    scale = jnp.exp2(-exponent(jnp.max(wide, axis=1, keepdims=True))) * STEPS
    sent_ref[:rows, :] = jnp.round(step * scale).astype(jnp.int32).astype(jnp.int16)
    power = exponent(in_lanes(wide, jnp.max)).astype(jnp.int32)
    rest = sent_ref.shape[1] - rows
    if rest:
        power = jnp.concatenate([power, jnp.zeros((1, rest), jnp.int32)], axis=1)
    sent_ref[rows:, :] = jnp.broadcast_to(power, (sent_ref.shape[0] - rows, sent_ref.shape[1])).astype(jnp.int16)


def code(pushed, positive, totals, k, gates):
    rows, channels = pushed.shape
    shape = jax.ShapeDtypeStruct((rows + 16, channels), jnp.int16)
    return call(
        functools.partial(code_kernel, k),
        "code",
        shape,
        2e8,
        in_specs=[NEAR] * 3 + [ANYWHERE] * len(gates),
    )(pushed, positive, totals, *gates)


def settle_kernel(turns, caps, note_ref, most_ref, held_ref, *refs):
    came = refs[: turns - 1]
    loss_ref, totals_ref, word_ref = refs[turns - 1 :]
    line = jnp.zeros(loss_ref.shape, F32)
    for t in range(turns):
        total = note_ref[t : t + 1, :]
        matched = note_ref[turns + t : turns + t + 1, :]
        for k in range(1, turns):
            ref = came[k - 1]
            total = total + ref[t ^ k : (t ^ k) + 1, :]
            matched = matched + ref[turns + (t ^ k) : turns + (t ^ k) + 1, :]
        totals_ref[t : t + 1, :] = total
        loss = jnp.log(total) + INV_TEMP - matched
        if t == 0:
            loss_ref[...] = loss
        line = line + loss
    over = (jnp.max(most_ref[...]) > caps[0]) | (jnp.max(held_ref[...]) > caps[1])
    word_ref[...] = jnp.zeros(word_ref.shape, F32)
    word_ref[0:1, 0:1] = jnp.sum(line, axis=1, keepdims=True)
    word_ref[1:2, :] = jnp.full((1, word_ref.shape[1]), jnp.where(over, 1.0, 0.0))


def settle(note, most, held, came, turns, caps):
    rows = note.shape[1]
    return call(
        functools.partial(settle_kernel, turns, caps),
        "settle",
        [
            jax.ShapeDtypeStruct((1, rows), F32),
            jax.ShapeDtypeStruct((-(-turns // 8) * 8, rows), F32),
            jax.ShapeDtypeStruct((8, 128), F32),
        ],
        1e8,
    )(note, most, held, *came)


def mean_kernel(queries, word_ref, came_ref, mean_ref, flag_ref):
    word = word_ref[...] + came_ref[...]
    mean_ref[0, 0] = jnp.sum(word[0:1, :]) * (1.0 / queries)
    flag_ref[0, 0] = (jnp.max(word[1:2, :]) > 0.5).astype(jnp.int32)


def mean(word, came, queries):
    return call(
        functools.partial(mean_kernel, queries),
        "mean",
        [jax.ShapeDtypeStruct((1, 1), F32), jax.ShapeDtypeStruct((1, 1), jnp.int32)],
        1e8,
        in_specs=[NEAR] * 2,
        out_specs=[SCALARS] * 2,
    )(word, came)


def finish_kernel(count, loss_in, raw_ref, positive_ref, own_ref, totals_ref, *refs):
    grad_ref, loss_ref = refs[count:]
    loss_ref[...] = loss_in[...]
    rows = raw_ref.shape[0]
    scales = [ref[rows : rows + 16, :rows].astype(jnp.int32).astype(F32)[0:1, :] for ref in refs[:count]]
    scales = [jnp.exp2(v) * (1.0 / STEPS) for v in scales]
    fill = -count % 128
    turned = jnp.concatenate(scales + [jnp.zeros((fill, rows), F32)], axis=0).T
    step = step_of(0, own_ref, positive_ref, totals_ref)
    for j in range(count):
        step = step + refs[j][:rows, :].astype(jnp.int32).astype(F32) * turned[:, j : j + 1]
    step = step * INV_TEMP
    raw = raw_ref[...].astype(F32)
    scale = lax.rsqrt(jnp.mean(raw * raw, axis=-1, keepdims=True) + EPSILON)
    inner = jnp.mean(step * raw, axis=-1, keepdims=True)
    grad_ref[...] = (step - raw * (scale * scale * inner)) * (scale / math.sqrt(raw.shape[1]))


def finish(loss, raw, positive, own, totals, parts):
    return call(
        functools.partial(finish_kernel, len(parts)),
        "finish",
        [jax.ShapeDtypeStruct(own.shape, F32), jax.ShapeDtypeStruct(loss.shape, F32)],
        5e8,
        in_specs=[NEAR] * (5 + len(parts)),
    )(loss, raw, positive, own, totals, *parts)


def on_device(features, patch_index, positive_index, bank):
    groups, copies = lax.axis_size("bank"), lax.axis_size("dp")
    place = lax.axis_index("bank")
    core = lax.axis_index("dp") % 2
    images, hw_dev, channels = features.shape
    queries_dp = images * patch_index.shape[1]
    owned = queries_dp // groups
    turns = groups // 2
    inner, outer = place % 2, place // 2
    bank_dev = bank.shape[0]
    across = [(b, b ^ 1) for b in range(groups)]
    swap = [(c, c ^ 1) for c in range(copies)]

    def turn(value, k):
        pairs = [(b, b ^ (2 * k)) for b in range(groups)]
        return lax.ppermute(value, "bank", pairs)

    def to_all(values):
        return [values[0]] + [turn(values[k], k) for k in [*range(2, turns), 1]]

    cap = capacity(queries_dp / groups / 2, queries_dp // 2, 4.0)
    half = bank_dev // 2
    relay = half * 2 // 8 // 16 * 16
    rest = half - 2 * relay
    row = (lax.axis_index("dp") // 2) % 2
    start = core * half // 16
    numbers = jnp.stack([place, start + row * (relay // 16), start + relay // 8])
    own_set, other_set, relay_out, rest_out = pick(features, patch_index, bank, numbers, relay, rest, owned, cap)
    from_side = lax.ppermute(other_set, "bank", across)
    relayed = lax.ppermute(relay_out, "bank", across)
    rest_in = lax.ppermute(rest_out, "bank", across)
    held_rows = jnp.concatenate([own_set, from_side])
    parts = to_all([held_rows] * turns)

    loc, most = locate(patch_index, place, groups, owned, cap, hw_dev, [from_side])
    over = [(c, c ^ 2) for c in range(copies)]
    from_row = lax.ppermute(after(relayed, loc), "dp", over)

    cap_pos = capacity(queries_dp / groups / 2, queries_dp // 2, 5.0)
    index = positive_index.reshape(images, -1)
    numbers = jnp.stack([place, core, row])
    near_keys, own_keys, listed, key_loc, held = bring_keys(
        index, bank, numbers, groups, owned, cap_pos, relay, [from_side]
    )

    here = place.reshape(1)
    early_rows = early(here, loc, parts[:2], turns, [])
    query, raw, blocks = arrange(here, loc, early_rows, parts[2:], 4 * cap, turns, [near_keys, key_loc])

    far_keys = []
    for part in (relayed, from_row, rest_in):
        part = after(part, query)
        far_keys += [part, lax.ppermute(part, "dp", swap)]
    total, pushed = first(query, near_keys, turns, [far_keys[0], far_keys[2], far_keys[4]])
    note, positive = far_totals(here, key_loc, query, total, own_keys, listed, far_keys, turns)
    came = to_all([note] * turns)
    came = [came[-1], *came[1:-1]]
    loss, totals, word = settle(note, most, held, came, turns, (cap, cap_pos))
    moved = [None] * turns
    order = [*range(2, turns)]
    order.insert(1, 1)
    whole = {k: last(blocks[k], pushed[k], far_keys, note) for k in order[:3]}
    words = [word]
    for axis, step in [("dp", 1), ("bank", 1)] + [("dp", 1 << i) for i in range(1, copies.bit_length() - 1)]:
        pairs = [(i, i ^ step) for i in range(lax.axis_size(axis))]
        came_word = lax.ppermute(words[-1], axis, pairs)
        words.append(words[-1] + came_word)
    gates = [totals]
    for k in order:
        if k not in whole:
            whole[k] = last(blocks[k], pushed[k], far_keys, gates[0])
        sent = code(whole[k], positive[k], totals, k, gates)
        moved[k] = turn(sent, k)
        gates = [sent, words[1]]
    own = last(blocks[0], pushed[0], far_keys, words[-2])
    mean_loss, flag = mean(words[-2], came_word, queries_dp * copies)
    ready = [loss, raw, positive[0], own, totals, *moved[1:]]

    def usual(given, ready, mean_loss):
        grad, loss = finish(*ready[:5], ready[5:])
        return (loss.reshape(owned), grad, mean_loss)

    return lax.cond(
        flag.reshape(()) > 0,
        lambda given, ready, mean_loss: plain(*given),
        usual,
        [features, patch_index, positive_index, bank],
        ready,
        mean_loss.reshape(()),
    )


def solution(mesh):
    in_specs = (P("dp", "bank", None), P("dp", None), P("dp"), P("bank", None))
    out_specs = (P(("dp", "bank")), P(("dp", "bank"), None), P())
    turns = mesh.shape["bank"] // 2
    paired = turns > 1 and turns & (turns - 1) == 0 and mesh.shape["bank"] % 2 == 0
    copies = mesh.shape["dp"]
    paired = paired and copies > 2 and copies & (copies - 1) == 0
    return jax.shard_map(
        on_device if paired else plain, mesh=mesh, in_specs=in_specs, out_specs=out_specs, check_vma=False
    )
```

```python
import functools
import math

import jax
import jax.numpy as jnp
from jax import lax
from jax.experimental import pallas as pl
from jax.experimental.pallas import tpu as pltpu
from jax.sharding import PartitionSpec as P

SOFTMAX_TEMP = 0.07
EPSILON = 1e-05
INV_TEMP = 1.0 / SOFTMAX_TEMP
RATE = INV_TEMP * math.log2(math.e)
STEPS = 32700.0
F32 = jnp.float32
BF16 = jnp.bfloat16
NT = (((1,), (1,)), ((), ()))


def normalize(values):
    scale = lax.rsqrt(jnp.mean(values * values, axis=-1, keepdims=True) + EPSILON)
    return values * scale / math.sqrt(values.shape[-1])


def ring_sum(value, axis):
    size = lax.axis_size(axis)
    pairs = [(i, (i + 1) % size) for i in range(size)]

    def step(_, carry):
        moving, total = carry
        moving = lax.ppermute(moving, axis, pairs)
        return (moving, total + moving)

    return lax.fori_loop(0, size - 1, step, (value, value))[1]


def plain(features, patch_index, positive_index, bank):
    groups = lax.axis_size("bank")
    place = lax.axis_index("bank")
    images, hw_dev, channels = features.shape
    queries_dp = images * patch_index.shape[1]
    owned_rows = queries_dp // groups
    local_pos = patch_index - place * hw_dev
    onehot = (local_pos[:, :, None] == jnp.arange(hw_dev, dtype=jnp.int32)[None, None, :]).astype(BF16)
    picked = jnp.einsum("iph,ihc->ipc", onehot, features, preferred_element_type=F32)
    raw_all = ring_sum(picked.reshape(queries_dp, channels), "bank")
    query_vector = normalize(raw_all).astype(BF16)
    raw_own = lax.dynamic_slice_in_dim(raw_all, place * owned_rows, owned_rows, 0)
    bank_dev = bank.shape[0]
    block_keys = math.gcd(bank_dev, 512)

    def visit(index, carry):
        exponent_sum, weighted = carry
        block = lax.dynamic_slice_in_dim(bank, index * block_keys, block_keys, 0)
        logit = lax.dot_general(query_vector, block, NT, preferred_element_type=F32) / SOFTMAX_TEMP
        terms = jnp.exp(logit - INV_TEMP)
        exponent_sum = exponent_sum + jnp.sum(terms, axis=1)
        weighted = weighted + jnp.dot(terms.astype(BF16), block, preferred_element_type=F32)
        return (exponent_sum, weighted)

    start = (jnp.zeros((queries_dp,), F32), jnp.zeros((queries_dp, channels), F32))
    exponent_sum, weighted = lax.fori_loop(0, bank_dev // block_keys, visit, start)
    key_pos = positive_index - place * bank_dev
    inside = (key_pos >= 0) & (key_pos < bank_dev)
    rows_pos = jnp.clip(key_pos, 0, bank_dev - 1)
    positive_key = bank[rows_pos].astype(F32) * inside[:, None].astype(F32)
    matched = jnp.sum(query_vector.astype(F32) * positive_key, axis=1) / SOFTMAX_TEMP
    own_sum, own_logit, own_weighted, own_positive = (
        lax.dynamic_slice_in_dim(ring_sum(v, "bank"), place * owned_rows, owned_rows, 0)
        for v in (exponent_sum, matched, weighted, positive_key)
    )
    step = (own_weighted / own_sum[:, None] - own_positive) / SOFTMAX_TEMP
    loss = jnp.log(own_sum) + INV_TEMP - own_logit
    _, pullback = jax.vjp(normalize, raw_own)
    query_grad = pullback(step)[0]
    count_all = queries_dp * lax.axis_size("dp")
    mean_loss = ring_sum(ring_sum(jnp.full((8, 128), jnp.sum(loss)), "bank"), "dp")[0, 0] / count_all
    return (loss, query_grad, mean_loss)


def cost(flops):
    return pl.CostEstimate(flops=int(flops), bytes_accessed=1 << 20, transcendentals=0)


def capacity(mean, least, sigmas):
    room = mean + sigmas * math.sqrt(mean)
    return min(least, -(-int(math.ceil(room)) // 16) * 16)


def call(kernel, name, out_shape, flops, room=16, **more):
    params = pltpu.CompilerParams(vmem_limit_bytes=room << 20)
    return pl.pallas_call(
        kernel, out_shape=out_shape, compiler_params=params, cost_estimate=cost(flops), name=name, **more
    )


ANYWHERE = pl.BlockSpec(memory_space=pl.ANY)


def after(value, *others):
    return call(
        lambda *refs: None,
        "after",
        jax.ShapeDtypeStruct(value.shape, value.dtype),
        0,
        in_specs=[ANYWHERE] * (1 + len(others)),
        out_specs=ANYWHERE,
        input_output_aliases={0: 0},
    )(value, *others)


def in_lanes(column_parts, reduce):
    return reduce(column_parts.T, axis=0, keepdims=True)


def ranks_of(code, codes):
    rows, lanes = code.shape
    batch = math.gcd(codes, 16)
    tall = batch * rows
    up = lax.broadcasted_iota(jnp.int32, (lanes, 2 * lanes), 0) <= lax.broadcasted_iota(
        jnp.int32, (lanes, 2 * lanes), 1
    )
    up = up.astype(F32).astype(BF16)
    above = lax.broadcasted_iota(jnp.int32, (tall, tall), 0)
    under = lax.broadcasted_iota(jnp.int32, (tall, tall), 1)
    low = ((above > under) & (above // rows == under // rows)).astype(F32).astype(BF16)
    ranks = jnp.full(code.shape, -1.0, F32)
    most = jnp.zeros((1, lanes), F32)
    for g in range(0, codes, batch):
        mask = jnp.concatenate([(code == g + b).astype(F32) for b in range(batch)], axis=0)
        sums = jnp.dot(mask.astype(BF16), up, preferred_element_type=F32)
        count = sums[:, lanes:]
        rank = sums[:, :lanes] + jnp.dot(low, count.astype(BF16), preferred_element_type=F32)
        rank = rank * mask
        for b in range(batch):
            part = slice(b * rows, (b + 1) * rows)
            ranks = ranks + rank[part]
            most = jnp.maximum(most, jnp.sum(count[part], axis=0, keepdims=True))
    return ranks.astype(jnp.int32), most


def parity_of(shape, owned):
    row = lax.broadcasted_iota(jnp.int32, shape, 0) * shape[1] + lax.broadcasted_iota(jnp.int32, shape, 1)
    return (row // owned) % 2


def by_owner(value, owned):
    rows, lanes = value.shape
    out = []
    for start in range(0, rows * lanes, owned):
        row, lane = divmod(start, lanes)
        if owned <= lanes:
            out.append(value[row : row + 1, lane : lane + owned])
        else:
            out.append(jnp.concatenate([value[row + i : row + i + 1] for i in range(owned // lanes)], axis=1))
    return jnp.concatenate(out, axis=0)


def row_at(ref, place_ref, k):
    return ref[pl.ds(((place_ref[0] // 2) ^ k) * 2 + place_ref[0] % 2, 1), :]


SCALARS = pl.BlockSpec(memory_space=pltpu.SMEM)
NEAR = pl.BlockSpec(memory_space=pltpu.VMEM)


def pick_kernel(
    owned, cap, place_ref, pos_ref, feat_ref, bank_ref, own_ref, other_ref, relay_ref, rest_ref, table, sems
):
    fetches = []
    for i, (ref, at) in enumerate([(relay_ref, place_ref[1]), (rest_ref, place_ref[2])]):
        span = pl.ds(pl.multiple_of(at * 16, 16), ref.shape[0])
        fetches.append(pltpu.make_async_copy(bank_ref.at[span], ref, sems.at[i]))
        fetches[-1].start()
    place = place_ref[0]
    images, patches = pos_ref.shape
    hw = feat_ref.shape[1]
    pos = pos_ref[...]
    mine = pos // hw == place
    parity = (parity_of(pos.shape, owned) + place) % 2
    code = jnp.where(mine, parity, 2)
    ranks, _ = ranks_of(code, 2)
    slot = ranks + parity * cap
    slot = jnp.where(mine & (ranks < cap), slot, -1)
    local = jnp.where(mine, pos - place * hw, -1)
    batch = math.gcd(images, max(1, 256 // patches))
    where_slot = lax.broadcasted_iota(jnp.int32, (2 * cap, batch * patches), 0)
    where_pos = lax.broadcasted_iota(jnp.int32, (batch * hw, batch * patches), 0)
    for i in range(0, images, batch):
        slots = jnp.concatenate([slot[i + b : i + b + 1, :] for b in range(batch)], axis=1)
        locals_ = jnp.concatenate(
            [jnp.where(local[i + b : i + b + 1, :] < 0, -1, local[i + b : i + b + 1, :] + b * hw) for b in range(batch)],
            axis=1,
        )
        chosen = (where_slot == slots).astype(F32).astype(BF16)
        spots = (where_pos == locals_).astype(F32).astype(BF16)
        part = lax.dot_general(chosen, spots, NT, preferred_element_type=F32)
        table[:, i * hw : (i + batch) * hw] = part.astype(BF16)
    rows = feat_ref[...].reshape(images * hw, feat_ref.shape[2])
    total = jnp.dot(table[...], rows, preferred_element_type=F32)
    own_ref[...] = total[:cap].astype(BF16)
    other_ref[...] = total[cap:].astype(BF16)
    for fetch in fetches:
        fetch.wait()


def pick(features, patch_index, bank, numbers, relay, rest, owned, cap):
    images, hw, channels = features.shape
    return call(
        functools.partial(pick_kernel, owned, cap),
        "pick",
        [
            jax.ShapeDtypeStruct((cap, channels), BF16),
            jax.ShapeDtypeStruct((cap, channels), BF16),
            jax.ShapeDtypeStruct((relay, channels), BF16),
            jax.ShapeDtypeStruct((rest, channels), BF16),
        ],
        3e9,
        in_specs=[SCALARS, NEAR, NEAR, ANYWHERE],
        scratch_shapes=[pltpu.VMEM((2 * cap, images * hw), BF16), pltpu.SemaphoreType.DMA((2,))],
    )(numbers, patch_index, features, bank)


def locate_kernel(groups, owned, cap, hw, gates, place_ref, pos_ref, *refs):
    loc_ref, most_ref = refs[gates:]
    place = place_ref[0]
    pos = pos_ref[...]
    holder = pos // hw
    ranks, most = ranks_of(holder * 2 + parity_of(pos.shape, owned), 2 * groups)
    most_ref[...] = jnp.broadcast_to(most, most_ref.shape)
    away = (place // 2) ^ (holder // 2)
    side = (holder % 2 + place) % 2
    stand = away // 2 + (away % 2) * (groups // 4)
    loc_ref[...] = by_owner((stand * 2 + side) * cap + ranks, owned)


def locate(patch_index, place, groups, owned, cap, hw, gates):
    return call(
        functools.partial(locate_kernel, groups, owned, cap, hw, len(gates)),
        "locate",
        [
            jax.ShapeDtypeStruct((groups, owned), jnp.int32),
            jax.ShapeDtypeStruct((8, patch_index.shape[1]), F32),
        ],
        1e9,
        in_specs=[SCALARS, NEAR] + [ANYWHERE] * len(gates),
    )(place.reshape(1), patch_index, *gates)


def keys_kernel(groups, owned, cap, relay, gates, place_ref, index_ref, bank_ref, *refs):
    near_ref, own_ref, list_ref, loc_ref, most_ref, sem = refs[gates:]
    fetch = pltpu.make_async_copy(bank_ref, near_ref, sem)
    fetch.start()
    place, core, line = place_ref[0], place_ref[1], place_ref[2]
    index = index_ref[...]
    keys = near_ref.shape[0]
    holder = index // keys
    parity = parity_of(index.shape, owned)
    ranks, most = ranks_of(holder * 2 + parity, 2 * groups)
    most_ref[...] = jnp.broadcast_to(most, most_ref.shape)
    mine, theirs = holder == place, holder == (place ^ 1)
    loc_ref[...] = by_owner(jnp.where(mine, ranks, jnp.where(theirs, ranks + cap, -1)), owned)
    slot = jnp.where(theirs, ranks + cap, ranks)
    slot = jnp.where((mine | theirs) & (ranks < cap) & (parity == place % 2), slot, -1)
    half = keys // 2
    rest = half - 2 * relay
    far = index - (place ^ 1) * keys
    other = jnp.where(far // half == core, 0, 1)
    offset = far % half
    strip = jnp.where(offset // relay == line, 0, 1)
    far = jnp.where(
        offset < 2 * relay,
        (strip * 2 + other) * relay + offset % relay,
        4 * relay + other * rest + offset - 2 * relay,
    )
    local = (jnp.where(mine, index - place * keys, far) + 1).astype(F32)
    rows, lanes = index.shape
    where_slot = lax.broadcasted_iota(jnp.int32, (2 * cap, lanes), 0)
    listed = jnp.zeros((2 * cap, lanes), F32)
    for i in range(rows):
        listed = listed + jnp.where(where_slot == slot[i : i + 1, :], local[i : i + 1, :], 0.0)
    listed = jnp.sum(listed, axis=1, keepdims=True).astype(jnp.int32) - 1
    list_ref[...] = listed[cap:]
    fetch.wait()
    own_ref[...] = listed_rows(listed[:cap], [near_ref]).astype(BF16)


def listed_rows(listed, parts):
    total = jnp.zeros((listed.shape[0], parts[0].shape[1]), F32)
    start = 0
    for ref in parts:
        sub = math.gcd(ref.shape[0], 256)
        lane = lax.broadcasted_iota(jnp.int32, (listed.shape[0], sub), 1)
        for at in range(0, ref.shape[0], sub):
            table = (lane + (start + at) == listed).astype(F32).astype(BF16)
            total = total + jnp.dot(table, ref[at : at + sub, :], preferred_element_type=F32)
        start += ref.shape[0]
    return total


def bring_keys(index, bank, numbers, groups, owned, cap, relay, gates):
    channels = bank.shape[1]
    return call(
        functools.partial(keys_kernel, groups, owned, cap, relay, len(gates)),
        "keys",
        [
            jax.ShapeDtypeStruct(bank.shape, BF16),
            jax.ShapeDtypeStruct((cap, channels), BF16),
            jax.ShapeDtypeStruct((cap, 1), jnp.int32),
            jax.ShapeDtypeStruct((groups, owned), jnp.int32),
            jax.ShapeDtypeStruct((8, index.shape[1]), F32),
        ],
        2e9,
        in_specs=[SCALARS, NEAR] + [ANYWHERE] * (1 + len(gates)),
        scratch_shapes=[pltpu.SemaphoreType.DMA],
    )(numbers, index, bank, *gates)


def column_of(row):
    return jnp.broadcast_to(row, (128, row.shape[1])).T[:, 0:1]


def columns_of(ref, place_ref, turns):
    rows = jnp.concatenate([row_at(ref, place_ref, k) for k in range(turns)], axis=0).astype(F32)
    rows = jnp.concatenate([rows, jnp.zeros((-turns % 128, rows.shape[1]), F32)], axis=0)
    return rows.T.astype(jnp.int32)


def chosen_rows(column, parts, at):
    total = jnp.zeros((column.shape[0], parts[0].shape[1]), F32)
    for ref in parts:
        lane = lax.broadcasted_iota(jnp.int32, (column.shape[0], ref.shape[0]), 1)
        table = (lane + at == column).astype(F32).astype(BF16)
        total = total + jnp.dot(table, ref[...], preferred_element_type=F32)
        at += ref.shape[0]
    return total


def early_kernel(turns, gates, place_ref, loc_ref, *refs):
    refs = refs[gates:]
    rows = loc_ref.shape[1]
    columns = columns_of(loc_ref, place_ref, turns)
    for k in range(turns):
        chosen = chosen_rows(columns[:, k : k + 1], refs[:-1], 0)
        refs[-1][k * rows : (k + 1) * rows, :] = chosen.astype(BF16)


def early(place, loc, parts, turns, gates):
    return call(
        functools.partial(early_kernel, turns, len(gates)),
        "early",
        jax.ShapeDtypeStruct((turns * loc.shape[1], parts[0].shape[1]), BF16),
        2e9,
        in_specs=[SCALARS, NEAR] + [ANYWHERE] * len(gates) + [NEAR] * len(parts),
    )(place, loc, *gates, *parts)


def arrange_kernel(turns, gates, at, place_ref, loc_ref, early_ref, *refs):
    refs = refs[gates:]
    rows = loc_ref.shape[1]
    parts, (query_ref, raw_ref), blocks = refs[: -2 - turns], refs[-2 - turns : -turns], refs[-turns:]
    columns = columns_of(loc_ref, place_ref, turns)
    for k in range(turns):
        span = slice(k * rows, (k + 1) * rows)
        raw = early_ref[span, :].astype(F32) + chosen_rows(columns[:, k : k + 1], parts, at)
        query = normalize(raw).astype(BF16)
        query_ref[span, :] = query
        blocks[k][...] = query
        if k == 0:
            raw_ref[...] = raw.astype(BF16)


def arrange(place, loc, early_rows, parts, at, turns, gates):
    rows, channels = loc.shape[1], parts[0].shape[1]
    out = call(
        functools.partial(arrange_kernel, turns, len(gates), at),
        "arrange",
        [jax.ShapeDtypeStruct((turns * rows, channels), BF16)]
        + [jax.ShapeDtypeStruct((rows, channels), BF16)] * (turns + 1),
        3e9,
        in_specs=[SCALARS] + [NEAR] * 2 + [ANYWHERE] * len(gates) + [NEAR] * len(parts),
    )(place, loc, early_rows, *gates, *parts)
    return out[0], out[1], out[2:]


def sweep(query, keys, total, pushed):
    sub = math.gcd(keys.shape[0], 1024)
    for at in range(0, keys.shape[0], sub):
        block = keys[at : at + sub, :]
        logit = lax.dot_general(query, block, NT, preferred_element_type=F32)
        terms = jnp.exp2(logit * RATE - RATE)
        if total is not None:
            for c in range(0, sub, 128):
                total = total + terms[:, c : c + 128]
        pushed = pushed + jnp.dot(terms.astype(BF16), block, preferred_element_type=F32)
    return total, pushed


def first_kernel(turns, gates, query_ref, keys_ref, *refs):
    total_ref, blocks = refs[gates], refs[gates + 1 :]
    rows = query_ref.shape[0] // turns
    for k in range(turns):
        part = slice(k * rows, (k + 1) * rows)
        total_ref[part, :], blocks[k][...] = sweep(
            query_ref[part, :], keys_ref, jnp.zeros((rows, 128), F32), jnp.zeros(blocks[k].shape, F32)
        )


def first(query, keys, turns, gates):
    rows, channels = query.shape
    out = call(
        functools.partial(first_kernel, turns, len(gates)),
        "first",
        [jax.ShapeDtypeStruct((rows, 128), F32)] + [jax.ShapeDtypeStruct((rows // turns, channels), F32)] * turns,
        8 * rows * keys.shape[0] * channels,
        room=24,
        in_specs=[pl.BlockSpec(memory_space=pltpu.VMEM)] * 2 + [ANYWHERE] * len(gates),
    )(query, keys, *gates)
    return out[0], out[1:]


def lane_sums(query, keys, total):
    sub = math.gcd(keys.shape[0], 256)
    for at in range(0, keys.shape[0], sub):
        logit = lax.dot_general(query, keys[at : at + sub, :], NT, preferred_element_type=F32)
        terms = jnp.exp2(logit * RATE - RATE)
        for c in range(0, sub, 128):
            total = total + terms[:, c : c + 128]
    return total


def far_kernel(count, turns, place_ref, loc_ref, query_ref, total_in, own_ref, list_ref, *refs):
    keys, note_ref, outs, side_ref = refs[:count], refs[count], refs[count + 1 : -1], refs[-1]
    rows = note_ref.shape[1]
    side_ref[...] = listed_rows(list_ref[...], keys).astype(BF16)
    total = total_in[...]
    for ref in keys:
        total = lane_sums(query_ref[...], ref, total)
    note_ref[...] = jnp.zeros(note_ref.shape, F32)
    columns = columns_of(loc_ref, place_ref, turns)
    for t in range(turns):
        part = slice(t * rows, (t + 1) * rows)
        note_ref[t : t + 1, :] = in_lanes(total[part], jnp.sum)
        positive = chosen_rows(columns[:, t : t + 1], [own_ref, side_ref], 0)
        outs[t][...] = positive.astype(BF16)
        product = query_ref[part, :].astype(F32) * positive
        matched = in_lanes(sum(product[:, c : c + 128] for c in range(0, product.shape[1], 128)), jnp.sum)
        note_ref[turns + t : turns + t + 1, :] = matched / SOFTMAX_TEMP


def far_totals(place, loc, query, total, own, listed, keys, turns):
    lines = -(-2 * turns // 8) * 8
    rows, channels = query.shape[0] // turns, query.shape[1]
    out = call(
        functools.partial(far_kernel, len(keys), turns),
        "far",
        [jax.ShapeDtypeStruct((lines, rows), F32)] + [jax.ShapeDtypeStruct((rows, channels), BF16)] * turns,
        2 * query.shape[0] * sum(k.shape[0] for k in keys) * channels,
        room=24,
        in_specs=[SCALARS] + [NEAR] * (5 + len(keys)),
        scratch_shapes=[pltpu.VMEM(own.shape, BF16)],
    )(place, loc, query, total, own, listed, *keys)
    return out[0], out[1:]


def exponent(size):
    return jnp.ceil(jnp.log2(jnp.maximum(size, 1e-30)))


def last_kernel(query_ref, pushed_in, gate_ref, *refs):
    pushed = pushed_in[...]
    for ref in refs[:-1]:
        _, pushed = sweep(query_ref[...], ref, None, pushed)
    refs[-1][...] = pushed


def last(query, pushed, keys, gate):
    rows, channels = query.shape
    return call(
        last_kernel,
        "last",
        jax.ShapeDtypeStruct((rows, channels), F32),
        4 * rows * sum(v.shape[0] for v in keys) * channels,
        in_specs=[pl.BlockSpec(memory_space=pltpu.VMEM)] * 2 + [ANYWHERE] + [pl.BlockSpec(memory_space=pltpu.VMEM)] * len(keys),
    )(query, pushed, gate, *keys)


def step_of(k, pushed_ref, positive_ref, totals_ref):
    return pushed_ref[...] / column_of(totals_ref[k : k + 1, :]) - positive_ref[...].astype(F32)


def code_kernel(k, pushed_ref, positive_ref, totals_ref, *refs):
    sent_ref = refs[-1]
    step = step_of(k, pushed_ref, positive_ref, totals_ref)
    size = jnp.abs(step)
    wide = size[:, :128]
    for c in range(128, size.shape[1], 128):
        wide = jnp.maximum(wide, size[:, c : c + 128])
    rows = step.shape[0]
    scale = jnp.exp2(-exponent(jnp.max(wide, axis=1, keepdims=True))) * STEPS
    sent_ref[:rows, :] = jnp.round(step * scale).astype(jnp.int32).astype(jnp.int16)
    power = exponent(in_lanes(wide, jnp.max)).astype(jnp.int32)
    rest = sent_ref.shape[1] - rows
    if rest:
        power = jnp.concatenate([power, jnp.zeros((1, rest), jnp.int32)], axis=1)
    sent_ref[rows:, :] = jnp.broadcast_to(power, (sent_ref.shape[0] - rows, sent_ref.shape[1])).astype(jnp.int16)


def code(pushed, positive, totals, k, gates):
    rows, channels = pushed.shape
    shape = jax.ShapeDtypeStruct((rows + 16, channels), jnp.int16)
    return call(
        functools.partial(code_kernel, k),
        "code",
        shape,
        2e8,
        in_specs=[NEAR] * 3 + [ANYWHERE] * len(gates),
    )(pushed, positive, totals, *gates)


def settle_kernel(turns, caps, note_ref, most_ref, held_ref, *refs):
    came = refs[: turns - 1]
    loss_ref, totals_ref, word_ref = refs[turns - 1 :]
    line = jnp.zeros(loss_ref.shape, F32)
    for t in range(turns):
        total = note_ref[t : t + 1, :]
        matched = note_ref[turns + t : turns + t + 1, :]
        for k in range(1, turns):
            ref = came[k - 1]
            total = total + ref[t ^ k : (t ^ k) + 1, :]
            matched = matched + ref[turns + (t ^ k) : turns + (t ^ k) + 1, :]
        totals_ref[t : t + 1, :] = total
        loss = jnp.log(total) + INV_TEMP - matched
        if t == 0:
            loss_ref[...] = loss
        line = line + loss
    over = (jnp.max(most_ref[...]) > caps[0]) | (jnp.max(held_ref[...]) > caps[1])
    word_ref[...] = jnp.zeros(word_ref.shape, F32)
    word_ref[0:1, 0:1] = jnp.sum(line, axis=1, keepdims=True)
    word_ref[1:2, :] = jnp.full((1, word_ref.shape[1]), jnp.where(over, 1.0, 0.0))


def settle(note, most, held, came, turns, caps):
    rows = note.shape[1]
    return call(
        functools.partial(settle_kernel, turns, caps),
        "settle",
        [
            jax.ShapeDtypeStruct((1, rows), F32),
            jax.ShapeDtypeStruct((-(-turns // 8) * 8, rows), F32),
            jax.ShapeDtypeStruct((8, 128), F32),
        ],
        1e8,
    )(note, most, held, *came)


def mean_kernel(queries, word_ref, came_ref, mean_ref, flag_ref):
    word = word_ref[...] + came_ref[...]
    mean_ref[0, 0] = jnp.sum(word[0:1, :]) * (1.0 / queries)
    flag_ref[0, 0] = (jnp.max(word[1:2, :]) > 0.5).astype(jnp.int32)


def mean(word, came, queries):
    return call(
        functools.partial(mean_kernel, queries),
        "mean",
        [jax.ShapeDtypeStruct((1, 1), F32), jax.ShapeDtypeStruct((1, 1), jnp.int32)],
        1e8,
        in_specs=[NEAR] * 2,
        out_specs=[SCALARS] * 2,
    )(word, came)


def finish_kernel(count, loss_in, raw_ref, positive_ref, own_ref, totals_ref, *refs):
    grad_ref, loss_ref = refs[count:]
    loss_ref[...] = loss_in[...]
    rows = raw_ref.shape[0]
    scales = [ref[rows : rows + 16, :rows].astype(jnp.int32).astype(F32)[0:1, :] for ref in refs[:count]]
    scales = [jnp.exp2(v) * (1.0 / STEPS) for v in scales]
    fill = -count % 128
    turned = jnp.concatenate(scales + [jnp.zeros((fill, rows), F32)], axis=0).T
    step = step_of(0, own_ref, positive_ref, totals_ref)
    for j in range(count):
        step = step + refs[j][:rows, :].astype(jnp.int32).astype(F32) * turned[:, j : j + 1]
    step = step * INV_TEMP
    raw = raw_ref[...].astype(F32)
    scale = lax.rsqrt(jnp.mean(raw * raw, axis=-1, keepdims=True) + EPSILON)
    inner = jnp.mean(step * raw, axis=-1, keepdims=True)
    grad_ref[...] = (step - raw * (scale * scale * inner)) * (scale / math.sqrt(raw.shape[1]))


def finish(loss, raw, positive, own, totals, parts):
    return call(
        functools.partial(finish_kernel, len(parts)),
        "finish",
        [jax.ShapeDtypeStruct(own.shape, F32), jax.ShapeDtypeStruct(loss.shape, F32)],
        5e8,
        in_specs=[NEAR] * (5 + len(parts)),
    )(loss, raw, positive, own, totals, *parts)


def on_device(features, patch_index, positive_index, bank):
    groups, copies = lax.axis_size("bank"), lax.axis_size("dp")
    place = lax.axis_index("bank")
    core = lax.axis_index("dp") % 2
    images, hw_dev, channels = features.shape
    queries_dp = images * patch_index.shape[1]
    owned = queries_dp // groups
    turns = groups // 2
    inner, outer = place % 2, place // 2
    bank_dev = bank.shape[0]
    across = [(b, b ^ 1) for b in range(groups)]
    swap = [(c, c ^ 1) for c in range(copies)]

    def turn(value, k):
        pairs = [(b, b ^ (2 * k)) for b in range(groups)]
        return lax.ppermute(value, "bank", pairs)

    def to_all(values):
        return [values[0]] + [turn(values[k], k) for k in [*range(2, turns), 1]]

    cap = capacity(queries_dp / groups / 2, queries_dp // 2, 4.0)
    half = bank_dev // 2
    relay = half * 2 // 8 // 16 * 16
    rest = half - 2 * relay
    row = (lax.axis_index("dp") // 2) % 2
    start = core * half // 16
    numbers = jnp.stack([place, start + row * (relay // 16), start + relay // 8])
    own_set, other_set, relay_out, rest_out = pick(features, patch_index, bank, numbers, relay, rest, owned, cap)
    from_side = lax.ppermute(other_set, "bank", across)
    relayed = lax.ppermute(relay_out, "bank", across)
    rest_in = lax.ppermute(rest_out, "bank", across)
    held_rows = jnp.concatenate([own_set, from_side])
    parts = [held_rows]
    for k in range(1, turns):
        parts.append(turn(parts[k & (k - 1)], k & -k))
    parts = parts[::2] + parts[1::2]

    loc, most = locate(patch_index, place, groups, owned, cap, hw_dev, [from_side])
    over = [(c, c ^ 2) for c in range(copies)]
    from_row = lax.ppermute(after(relayed, loc), "dp", over)

    cap_pos = capacity(queries_dp / groups / 2, queries_dp // 2, 5.0)
    index = positive_index.reshape(images, -1)
    numbers = jnp.stack([place, core, row])
    near_keys, own_keys, listed, key_loc, held = bring_keys(
        index, bank, numbers, groups, owned, cap_pos, relay, [from_side]
    )

    here = place.reshape(1)
    early_rows = early(here, loc, parts[:2], turns, [])
    query, raw, blocks = arrange(here, loc, early_rows, parts[2:], 4 * cap, turns, [near_keys, key_loc])

    far_keys = []
    for part in (relayed, from_row, rest_in):
        part = after(part, query)
        far_keys += [part, lax.ppermute(part, "dp", swap)]
    total, pushed = first(query, near_keys, turns, [far_keys[0], far_keys[2], far_keys[4]])
    note, positive = far_totals(here, key_loc, query, total, own_keys, listed, far_keys, turns)
    came = to_all([note] * turns)
    came = [came[-1], *came[1:-1]]
    loss, totals, word = settle(note, most, held, came, turns, (cap, cap_pos))
    moved = [None] * turns
    order = [*range(2, turns)]
    order.insert(1, 1)
    whole = {k: last(blocks[k], pushed[k], far_keys, note) for k in order[:3]}
    words = [word]
    for axis, step in [("dp", 1), ("bank", 1)] + [("dp", 1 << i) for i in range(1, copies.bit_length() - 1)]:
        pairs = [(i, i ^ step) for i in range(lax.axis_size(axis))]
        came_word = lax.ppermute(words[-1], axis, pairs)
        words.append(words[-1] + came_word)
    gates = [totals]
    for k in order:
        if k not in whole:
            whole[k] = last(blocks[k], pushed[k], far_keys, gates[0])
        sent = code(whole[k], positive[k], totals, k, gates)
        moved[k] = turn(sent, k)
        gates = [sent, words[1]]
    own = last(blocks[0], pushed[0], far_keys, words[-2])
    mean_loss, flag = mean(words[-2], came_word, queries_dp * copies)
    ready = [loss, raw, positive[0], own, totals, *moved[1:]]

    def usual(given, ready, mean_loss):
        grad, loss = finish(*ready[:5], ready[5:])
        return (loss.reshape(owned), grad, mean_loss)

    return lax.cond(
        flag.reshape(()) > 0,
        lambda given, ready, mean_loss: plain(*given),
        usual,
        [features, patch_index, positive_index, bank],
        ready,
        mean_loss.reshape(()),
    )


def solution(mesh):
    in_specs = (P("dp", "bank", None), P("dp", None), P("dp"), P("bank", None))
    out_specs = (P(("dp", "bank")), P(("dp", "bank"), None), P())
    turns = mesh.shape["bank"] // 2
    paired = turns > 2 and turns & (turns - 1) == 0 and mesh.shape["bank"] % 2 == 0
    copies = mesh.shape["dp"]
    paired = paired and copies > 2 and copies & (copies - 1) == 0
    return jax.shard_map(
        on_device if paired else plain, mesh=mesh, in_specs=in_specs, out_specs=out_specs, check_vma=False
    )
```

```python
import functools
import math

import jax
import jax.numpy as jnp
from jax import lax
from jax.experimental import pallas as pl
from jax.experimental.pallas import tpu as pltpu
from jax.sharding import PartitionSpec as P

SOFTMAX_TEMP = 0.07
EPSILON = 1e-05
INV_TEMP = 1.0 / SOFTMAX_TEMP
RATE = INV_TEMP * math.log2(math.e)
STEPS = 32700.0
F32 = jnp.float32
BF16 = jnp.bfloat16
NT = (((1,), (1,)), ((), ()))


def normalize(values):
    scale = lax.rsqrt(jnp.mean(values * values, axis=-1, keepdims=True) + EPSILON)
    return values * scale / math.sqrt(values.shape[-1])


def ring_sum(value, axis):
    size = lax.axis_size(axis)
    pairs = [(i, (i + 1) % size) for i in range(size)]

    def step(_, carry):
        moving, total = carry
        moving = lax.ppermute(moving, axis, pairs)
        return (moving, total + moving)

    return lax.fori_loop(0, size - 1, step, (value, value))[1]


def plain(features, patch_index, positive_index, bank):
    groups = lax.axis_size("bank")
    place = lax.axis_index("bank")
    images, hw_dev, channels = features.shape
    queries_dp = images * patch_index.shape[1]
    owned_rows = queries_dp // groups
    local_pos = patch_index - place * hw_dev
    onehot = (local_pos[:, :, None] == jnp.arange(hw_dev, dtype=jnp.int32)[None, None, :]).astype(BF16)
    picked = jnp.einsum("iph,ihc->ipc", onehot, features, preferred_element_type=F32)
    raw_all = ring_sum(picked.reshape(queries_dp, channels), "bank")
    query_vector = normalize(raw_all).astype(BF16)
    raw_own = lax.dynamic_slice_in_dim(raw_all, place * owned_rows, owned_rows, 0)
    bank_dev = bank.shape[0]
    block_keys = math.gcd(bank_dev, 512)

    def visit(index, carry):
        exponent_sum, weighted = carry
        block = lax.dynamic_slice_in_dim(bank, index * block_keys, block_keys, 0)
        logit = lax.dot_general(query_vector, block, NT, preferred_element_type=F32) / SOFTMAX_TEMP
        terms = jnp.exp(logit - INV_TEMP)
        exponent_sum = exponent_sum + jnp.sum(terms, axis=1)
        weighted = weighted + jnp.dot(terms.astype(BF16), block, preferred_element_type=F32)
        return (exponent_sum, weighted)

    start = (jnp.zeros((queries_dp,), F32), jnp.zeros((queries_dp, channels), F32))
    exponent_sum, weighted = lax.fori_loop(0, bank_dev // block_keys, visit, start)
    key_pos = positive_index - place * bank_dev
    inside = (key_pos >= 0) & (key_pos < bank_dev)
    rows_pos = jnp.clip(key_pos, 0, bank_dev - 1)
    positive_key = bank[rows_pos].astype(F32) * inside[:, None].astype(F32)
    matched = jnp.sum(query_vector.astype(F32) * positive_key, axis=1) / SOFTMAX_TEMP
    own_sum, own_logit, own_weighted, own_positive = (
        lax.dynamic_slice_in_dim(ring_sum(v, "bank"), place * owned_rows, owned_rows, 0)
        for v in (exponent_sum, matched, weighted, positive_key)
    )
    step = (own_weighted / own_sum[:, None] - own_positive) / SOFTMAX_TEMP
    loss = jnp.log(own_sum) + INV_TEMP - own_logit
    _, pullback = jax.vjp(normalize, raw_own)
    query_grad = pullback(step)[0]
    count_all = queries_dp * lax.axis_size("dp")
    mean_loss = ring_sum(ring_sum(jnp.full((8, 128), jnp.sum(loss)), "bank"), "dp")[0, 0] / count_all
    return (loss, query_grad, mean_loss)


def cost(flops):
    return pl.CostEstimate(flops=int(flops), bytes_accessed=1 << 20, transcendentals=0)


def capacity(mean, least, sigmas):
    room = mean + sigmas * math.sqrt(mean)
    return min(least, -(-int(math.ceil(room)) // 16) * 16)


def call(kernel, name, out_shape, flops, room=16, **more):
    params = pltpu.CompilerParams(vmem_limit_bytes=room << 20)
    return pl.pallas_call(
        kernel, out_shape=out_shape, compiler_params=params, cost_estimate=cost(flops), name=name, **more
    )


ANYWHERE = pl.BlockSpec(memory_space=pl.ANY)


def after(value, *others):
    return call(
        lambda *refs: None,
        "after",
        jax.ShapeDtypeStruct(value.shape, value.dtype),
        0,
        in_specs=[ANYWHERE] * (1 + len(others)),
        out_specs=ANYWHERE,
        input_output_aliases={0: 0},
    )(value, *others)


def in_lanes(column_parts, reduce):
    return reduce(column_parts.T, axis=0, keepdims=True)


def ranks_of(code, codes):
    rows, lanes = code.shape
    batch = math.gcd(codes, 16)
    tall = batch * rows
    up = lax.broadcasted_iota(jnp.int32, (lanes, 2 * lanes), 0) <= lax.broadcasted_iota(
        jnp.int32, (lanes, 2 * lanes), 1
    )
    up = up.astype(F32).astype(BF16)
    above = lax.broadcasted_iota(jnp.int32, (tall, tall), 0)
    under = lax.broadcasted_iota(jnp.int32, (tall, tall), 1)
    low = ((above > under) & (above // rows == under // rows)).astype(F32).astype(BF16)
    ranks = jnp.full(code.shape, -1.0, F32)
    most = jnp.zeros((1, lanes), F32)
    for g in range(0, codes, batch):
        mask = jnp.concatenate([(code == g + b).astype(F32) for b in range(batch)], axis=0)
        sums = jnp.dot(mask.astype(BF16), up, preferred_element_type=F32)
        count = sums[:, lanes:]
        rank = sums[:, :lanes] + jnp.dot(low, count.astype(BF16), preferred_element_type=F32)
        rank = rank * mask
        for b in range(batch):
            part = slice(b * rows, (b + 1) * rows)
            ranks = ranks + rank[part]
            most = jnp.maximum(most, jnp.sum(count[part], axis=0, keepdims=True))
    return ranks.astype(jnp.int32), most


def parity_of(shape, owned):
    row = lax.broadcasted_iota(jnp.int32, shape, 0) * shape[1] + lax.broadcasted_iota(jnp.int32, shape, 1)
    return (row // owned) % 2


def by_owner(value, owned):
    rows, lanes = value.shape
    out = []
    for start in range(0, rows * lanes, owned):
        row, lane = divmod(start, lanes)
        if owned <= lanes:
            out.append(value[row : row + 1, lane : lane + owned])
        else:
            out.append(jnp.concatenate([value[row + i : row + i + 1] for i in range(owned // lanes)], axis=1))
    return jnp.concatenate(out, axis=0)


def row_at(ref, place_ref, k):
    return ref[pl.ds(((place_ref[0] // 2) ^ k) * 2 + place_ref[0] % 2, 1), :]


SCALARS = pl.BlockSpec(memory_space=pltpu.SMEM)
NEAR = pl.BlockSpec(memory_space=pltpu.VMEM)


def pick_kernel(
    owned, cap, place_ref, pos_ref, feat_ref, bank_ref, own_ref, other_ref, relay_ref, rest_ref, table, sems
):
    fetches = []
    for i, (ref, at) in enumerate([(relay_ref, place_ref[1]), (rest_ref, place_ref[2])]):
        span = pl.ds(pl.multiple_of(at * 16, 16), ref.shape[0])
        fetches.append(pltpu.make_async_copy(bank_ref.at[span], ref, sems.at[i]))
        fetches[-1].start()
    place = place_ref[0]
    images, patches = pos_ref.shape
    hw = feat_ref.shape[1]
    pos = pos_ref[...]
    mine = pos // hw == place
    parity = (parity_of(pos.shape, owned) + place) % 2
    code = jnp.where(mine, parity, 2)
    ranks, _ = ranks_of(code, 2)
    slot = ranks + parity * cap
    slot = jnp.where(mine & (ranks < cap), slot, -1)
    local = jnp.where(mine, pos - place * hw, -1)
    batch = math.gcd(images, max(1, 256 // patches))
    where_slot = lax.broadcasted_iota(jnp.int32, (2 * cap, batch * patches), 0)
    where_pos = lax.broadcasted_iota(jnp.int32, (batch * hw, batch * patches), 0)
    for i in range(0, images, batch):
        slots = jnp.concatenate([slot[i + b : i + b + 1, :] for b in range(batch)], axis=1)
        locals_ = jnp.concatenate(
            [jnp.where(local[i + b : i + b + 1, :] < 0, -1, local[i + b : i + b + 1, :] + b * hw) for b in range(batch)],
            axis=1,
        )
        chosen = (where_slot == slots).astype(F32).astype(BF16)
        spots = (where_pos == locals_).astype(F32).astype(BF16)
        part = lax.dot_general(chosen, spots, NT, preferred_element_type=F32)
        table[:, i * hw : (i + batch) * hw] = part.astype(BF16)
    rows = feat_ref[...].reshape(images * hw, feat_ref.shape[2])
    total = jnp.dot(table[...], rows, preferred_element_type=F32)
    own_ref[...] = total[:cap].astype(BF16)
    other_ref[...] = total[cap:].astype(BF16)
    for fetch in fetches:
        fetch.wait()


def pick(features, patch_index, bank, numbers, relay, rest, owned, cap):
    images, hw, channels = features.shape
    return call(
        functools.partial(pick_kernel, owned, cap),
        "pick",
        [
            jax.ShapeDtypeStruct((cap, channels), BF16),
            jax.ShapeDtypeStruct((cap, channels), BF16),
            jax.ShapeDtypeStruct((relay, channels), BF16),
            jax.ShapeDtypeStruct((rest, channels), BF16),
        ],
        3e9,
        in_specs=[SCALARS, NEAR, NEAR, ANYWHERE],
        scratch_shapes=[pltpu.VMEM((2 * cap, images * hw), BF16), pltpu.SemaphoreType.DMA((2,))],
    )(numbers, patch_index, features, bank)


def locate_kernel(groups, owned, cap, hw, gates, place_ref, pos_ref, *refs):
    loc_ref, most_ref = refs[gates:]
    place = place_ref[0]
    pos = pos_ref[...]
    holder = pos // hw
    ranks, most = ranks_of(holder * 2 + parity_of(pos.shape, owned), 2 * groups)
    most_ref[...] = jnp.broadcast_to(most, most_ref.shape)
    away = (place // 2) ^ (holder // 2)
    side = (holder % 2 + place) % 2
    stand = away // 2 + (away % 2) * (groups // 4)
    loc_ref[...] = by_owner((stand * 2 + side) * cap + ranks, owned)


def locate(patch_index, place, groups, owned, cap, hw, gates):
    return call(
        functools.partial(locate_kernel, groups, owned, cap, hw, len(gates)),
        "locate",
        [
            jax.ShapeDtypeStruct((groups, owned), jnp.int32),
            jax.ShapeDtypeStruct((8, patch_index.shape[1]), F32),
        ],
        1e9,
        in_specs=[SCALARS, NEAR] + [ANYWHERE] * len(gates),
    )(place.reshape(1), patch_index, *gates)


def keys_kernel(groups, owned, cap, relay, gates, place_ref, index_ref, bank_ref, *refs):
    near_ref, own_ref, list_ref, loc_ref, most_ref, sem = refs[gates:]
    fetch = pltpu.make_async_copy(bank_ref, near_ref, sem)
    fetch.start()
    place, core, line = place_ref[0], place_ref[1], place_ref[2]
    index = index_ref[...]
    keys = near_ref.shape[0]
    holder = index // keys
    parity = parity_of(index.shape, owned)
    ranks, most = ranks_of(holder * 2 + parity, 2 * groups)
    most_ref[...] = jnp.broadcast_to(most, most_ref.shape)
    mine, theirs = holder == place, holder == (place ^ 1)
    loc_ref[...] = by_owner(jnp.where(mine, ranks, jnp.where(theirs, ranks + cap, -1)), owned)
    slot = jnp.where(theirs, ranks + cap, ranks)
    slot = jnp.where((mine | theirs) & (ranks < cap) & (parity == place % 2), slot, -1)
    half = keys // 2
    rest = half - 2 * relay
    far = index - (place ^ 1) * keys
    other = jnp.where(far // half == core, 0, 1)
    offset = far % half
    strip = jnp.where(offset // relay == line, 0, 1)
    far = jnp.where(
        offset < 2 * relay,
        (strip * 2 + other) * relay + offset % relay,
        4 * relay + other * rest + offset - 2 * relay,
    )
    local = (jnp.where(mine, index - place * keys, far) + 1).astype(F32)
    rows, lanes = index.shape
    where_slot = lax.broadcasted_iota(jnp.int32, (2 * cap, lanes), 0)
    listed = jnp.zeros((2 * cap, lanes), F32)
    for i in range(rows):
        listed = listed + jnp.where(where_slot == slot[i : i + 1, :], local[i : i + 1, :], 0.0)
    listed = jnp.sum(listed, axis=1, keepdims=True).astype(jnp.int32) - 1
    list_ref[...] = listed[cap:]
    fetch.wait()
    own_ref[...] = listed_rows(listed[:cap], [near_ref]).astype(BF16)


def listed_rows(listed, parts):
    total = jnp.zeros((listed.shape[0], parts[0].shape[1]), F32)
    start = 0
    for ref in parts:
        sub = math.gcd(ref.shape[0], 256)
        lane = lax.broadcasted_iota(jnp.int32, (listed.shape[0], sub), 1)
        for at in range(0, ref.shape[0], sub):
            table = (lane + (start + at) == listed).astype(F32).astype(BF16)
            total = total + jnp.dot(table, ref[at : at + sub, :], preferred_element_type=F32)
        start += ref.shape[0]
    return total


def bring_keys(index, bank, numbers, groups, owned, cap, relay, gates):
    channels = bank.shape[1]
    return call(
        functools.partial(keys_kernel, groups, owned, cap, relay, len(gates)),
        "keys",
        [
            jax.ShapeDtypeStruct(bank.shape, BF16),
            jax.ShapeDtypeStruct((cap, channels), BF16),
            jax.ShapeDtypeStruct((cap, 1), jnp.int32),
            jax.ShapeDtypeStruct((groups, owned), jnp.int32),
            jax.ShapeDtypeStruct((8, index.shape[1]), F32),
        ],
        2e9,
        in_specs=[SCALARS, NEAR] + [ANYWHERE] * (1 + len(gates)),
        scratch_shapes=[pltpu.SemaphoreType.DMA],
    )(numbers, index, bank, *gates)


def column_of(row):
    return jnp.broadcast_to(row, (128, row.shape[1])).T[:, 0:1]


def columns_of(ref, place_ref, turns):
    rows = jnp.concatenate([row_at(ref, place_ref, k) for k in range(turns)], axis=0).astype(F32)
    rows = jnp.concatenate([rows, jnp.zeros((-turns % 128, rows.shape[1]), F32)], axis=0)
    return rows.T.astype(jnp.int32)


def chosen_rows(column, parts, at):
    total = jnp.zeros((column.shape[0], parts[0].shape[1]), F32)
    for ref in parts:
        lane = lax.broadcasted_iota(jnp.int32, (column.shape[0], ref.shape[0]), 1)
        table = (lane + at == column).astype(F32).astype(BF16)
        total = total + jnp.dot(table, ref[...], preferred_element_type=F32)
        at += ref.shape[0]
    return total


def early_kernel(turns, gates, place_ref, loc_ref, *refs):
    refs = refs[gates:]
    rows = loc_ref.shape[1]
    columns = columns_of(loc_ref, place_ref, turns)
    for k in range(turns):
        chosen = chosen_rows(columns[:, k : k + 1], refs[:-1], 0)
        refs[-1][k * rows : (k + 1) * rows, :] = chosen.astype(BF16)


def early(place, loc, parts, turns, gates):
    return call(
        functools.partial(early_kernel, turns, len(gates)),
        "early",
        jax.ShapeDtypeStruct((turns * loc.shape[1], parts[0].shape[1]), BF16),
        2e9,
        in_specs=[SCALARS, NEAR] + [ANYWHERE] * len(gates) + [NEAR] * len(parts),
    )(place, loc, *gates, *parts)


def arrange_kernel(turns, gates, at, place_ref, loc_ref, early_ref, *refs):
    refs = refs[gates:]
    rows = loc_ref.shape[1]
    parts, (query_ref, raw_ref), blocks = refs[: -2 - turns], refs[-2 - turns : -turns], refs[-turns:]
    columns = columns_of(loc_ref, place_ref, turns)
    for k in range(turns):
        span = slice(k * rows, (k + 1) * rows)
        raw = early_ref[span, :].astype(F32) + chosen_rows(columns[:, k : k + 1], parts, at)
        query = normalize(raw).astype(BF16)
        query_ref[span, :] = query
        blocks[k][...] = query
        if k == 0:
            raw_ref[...] = raw.astype(BF16)


def arrange(place, loc, early_rows, parts, at, turns, gates):
    rows, channels = loc.shape[1], parts[0].shape[1]
    out = call(
        functools.partial(arrange_kernel, turns, len(gates), at),
        "arrange",
        [jax.ShapeDtypeStruct((turns * rows, channels), BF16)]
        + [jax.ShapeDtypeStruct((rows, channels), BF16)] * (turns + 1),
        3e9,
        in_specs=[SCALARS] + [NEAR] * 2 + [ANYWHERE] * len(gates) + [NEAR] * len(parts),
    )(place, loc, early_rows, *gates, *parts)
    return out[0], out[1], out[2:]


def sweep(query, keys, total, pushed):
    sub = math.gcd(keys.shape[0], 1024)
    for at in range(0, keys.shape[0], sub):
        block = keys[at : at + sub, :]
        logit = lax.dot_general(query, block, NT, preferred_element_type=F32)
        terms = jnp.exp2(logit * RATE - RATE)
        if total is not None:
            for c in range(0, sub, 128):
                total = total + terms[:, c : c + 128]
        pushed = pushed + jnp.dot(terms.astype(BF16), block, preferred_element_type=F32)
    return total, pushed


def first_kernel(turns, gates, query_ref, keys_ref, *refs):
    total_ref, blocks = refs[gates], refs[gates + 1 :]
    rows = query_ref.shape[0] // turns
    for k in range(turns):
        part = slice(k * rows, (k + 1) * rows)
        total_ref[part, :], blocks[k][...] = sweep(
            query_ref[part, :], keys_ref, jnp.zeros((rows, 128), F32), jnp.zeros(blocks[k].shape, F32)
        )


def first(query, keys, turns, gates):
    rows, channels = query.shape
    out = call(
        functools.partial(first_kernel, turns, len(gates)),
        "first",
        [jax.ShapeDtypeStruct((rows, 128), F32)] + [jax.ShapeDtypeStruct((rows // turns, channels), F32)] * turns,
        8 * rows * keys.shape[0] * channels,
        room=24,
        in_specs=[pl.BlockSpec(memory_space=pltpu.VMEM)] * 2 + [ANYWHERE] * len(gates),
    )(query, keys, *gates)
    return out[0], out[1:]


def lane_sums(query, keys, total):
    sub = math.gcd(keys.shape[0], 256)
    for at in range(0, keys.shape[0], sub):
        logit = lax.dot_general(query, keys[at : at + sub, :], NT, preferred_element_type=F32)
        terms = jnp.exp2(logit * RATE - RATE)
        for c in range(0, sub, 128):
            total = total + terms[:, c : c + 128]
    return total


def far_kernel(count, turns, place_ref, loc_ref, query_ref, total_in, own_ref, list_ref, *refs):
    keys, note_ref, outs, side_ref = refs[:count], refs[count], refs[count + 1 : -1], refs[-1]
    rows = note_ref.shape[1]
    cap = own_ref.shape[0]
    side_ref[:cap, :] = own_ref[...]
    side_ref[cap:, :] = listed_rows(list_ref[...], keys).astype(BF16)
    total = total_in[...]
    for ref in keys:
        total = lane_sums(query_ref[...], ref, total)
    note_ref[...] = jnp.zeros(note_ref.shape, F32)
    columns = columns_of(loc_ref, place_ref, turns)
    for t in range(turns):
        part = slice(t * rows, (t + 1) * rows)
        note_ref[t : t + 1, :] = in_lanes(total[part], jnp.sum)
        positive = chosen_rows(columns[:, t : t + 1], [side_ref], 0)
        outs[t][...] = positive.astype(BF16)
        product = query_ref[part, :].astype(F32) * positive
        matched = in_lanes(sum(product[:, c : c + 128] for c in range(0, product.shape[1], 128)), jnp.sum)
        note_ref[turns + t : turns + t + 1, :] = matched / SOFTMAX_TEMP


def far_totals(place, loc, query, total, own, listed, keys, turns):
    lines = -(-2 * turns // 8) * 8
    rows, channels = query.shape[0] // turns, query.shape[1]
    out = call(
        functools.partial(far_kernel, len(keys), turns),
        "far",
        [jax.ShapeDtypeStruct((lines, rows), F32)] + [jax.ShapeDtypeStruct((rows, channels), BF16)] * turns,
        2 * query.shape[0] * sum(k.shape[0] for k in keys) * channels,
        room=24,
        in_specs=[SCALARS] + [NEAR] * (5 + len(keys)),
        scratch_shapes=[pltpu.VMEM((2 * own.shape[0], channels), BF16)],
    )(place, loc, query, total, own, listed, *keys)
    return out[0], out[1:]


def exponent(size):
    return jnp.ceil(jnp.log2(jnp.maximum(size, 1e-30)))


def last_kernel(query_ref, pushed_in, gate_ref, *refs):
    pushed = pushed_in[...]
    for ref in refs[:-1]:
        _, pushed = sweep(query_ref[...], ref, None, pushed)
    refs[-1][...] = pushed


def last(query, pushed, keys, gate):
    rows, channels = query.shape
    return call(
        last_kernel,
        "last",
        jax.ShapeDtypeStruct((rows, channels), F32),
        4 * rows * sum(v.shape[0] for v in keys) * channels,
        in_specs=[pl.BlockSpec(memory_space=pltpu.VMEM)] * 2 + [ANYWHERE] + [pl.BlockSpec(memory_space=pltpu.VMEM)] * len(keys),
    )(query, pushed, gate, *keys)


def step_of(k, pushed_ref, positive_ref, totals_ref):
    return pushed_ref[...] / column_of(totals_ref[k : k + 1, :]) - positive_ref[...].astype(F32)


def code_kernel(k, pushed_ref, positive_ref, totals_ref, *refs):
    sent_ref = refs[-1]
    step = step_of(k, pushed_ref, positive_ref, totals_ref)
    size = jnp.abs(step)
    wide = size[:, :128]
    for c in range(128, size.shape[1], 128):
        wide = jnp.maximum(wide, size[:, c : c + 128])
    rows = step.shape[0]
    scale = jnp.exp2(-exponent(jnp.max(wide, axis=1, keepdims=True))) * STEPS
    sent_ref[:rows, :] = jnp.round(step * scale).astype(jnp.int32).astype(jnp.int16)
    power = exponent(in_lanes(wide, jnp.max)).astype(jnp.int32)
    rest = sent_ref.shape[1] - rows
    if rest:
        power = jnp.concatenate([power, jnp.zeros((1, rest), jnp.int32)], axis=1)
    sent_ref[rows:, :] = jnp.broadcast_to(power, (sent_ref.shape[0] - rows, sent_ref.shape[1])).astype(jnp.int16)


def code(pushed, positive, totals, k, gates):
    rows, channels = pushed.shape
    shape = jax.ShapeDtypeStruct((rows + 16, channels), jnp.int16)
    return call(
        functools.partial(code_kernel, k),
        "code",
        shape,
        2e8,
        in_specs=[NEAR] * 3 + [ANYWHERE] * len(gates),
    )(pushed, positive, totals, *gates)


def settle_kernel(turns, caps, note_ref, most_ref, held_ref, *refs):
    came = refs[: turns - 1]
    loss_ref, totals_ref, word_ref = refs[turns - 1 :]
    line = jnp.zeros(loss_ref.shape, F32)
    for t in range(turns):
        total = note_ref[t : t + 1, :]
        matched = note_ref[turns + t : turns + t + 1, :]
        for k in range(1, turns):
            ref = came[k - 1]
            total = total + ref[t ^ k : (t ^ k) + 1, :]
            matched = matched + ref[turns + (t ^ k) : turns + (t ^ k) + 1, :]
        totals_ref[t : t + 1, :] = total
        loss = jnp.log(total) + INV_TEMP - matched
        if t == 0:
            loss_ref[...] = loss
        line = line + loss
    over = (jnp.max(most_ref[...]) > caps[0]) | (jnp.max(held_ref[...]) > caps[1])
    word_ref[...] = jnp.zeros(word_ref.shape, F32)
    word_ref[0:1, 0:1] = jnp.sum(line, axis=1, keepdims=True)
    word_ref[1:2, :] = jnp.full((1, word_ref.shape[1]), jnp.where(over, 1.0, 0.0))


def settle(note, most, held, came, turns, caps):
    rows = note.shape[1]
    return call(
        functools.partial(settle_kernel, turns, caps),
        "settle",
        [
            jax.ShapeDtypeStruct((1, rows), F32),
            jax.ShapeDtypeStruct((-(-turns // 8) * 8, rows), F32),
            jax.ShapeDtypeStruct((8, 128), F32),
        ],
        1e8,
    )(note, most, held, *came)


def mean_kernel(queries, word_ref, came_ref, mean_ref, flag_ref):
    word = word_ref[...] + came_ref[...]
    mean_ref[0, 0] = jnp.sum(word[0:1, :]) * (1.0 / queries)
    flag_ref[0, 0] = (jnp.max(word[1:2, :]) > 0.5).astype(jnp.int32)


def mean(word, came, queries):
    return call(
        functools.partial(mean_kernel, queries),
        "mean",
        [jax.ShapeDtypeStruct((1, 1), F32), jax.ShapeDtypeStruct((1, 1), jnp.int32)],
        1e8,
        in_specs=[NEAR] * 2,
        out_specs=[SCALARS] * 2,
    )(word, came)


def finish_kernel(count, loss_in, raw_ref, positive_ref, own_ref, totals_ref, *refs):
    grad_ref, loss_ref = refs[count:]
    loss_ref[...] = loss_in[...]
    rows = raw_ref.shape[0]
    scales = [ref[rows : rows + 16, :rows].astype(jnp.int32).astype(F32)[0:1, :] for ref in refs[:count]]
    scales = [jnp.exp2(v) * (1.0 / STEPS) for v in scales]
    fill = -count % 128
    turned = jnp.concatenate(scales + [jnp.zeros((fill, rows), F32)], axis=0).T
    step = step_of(0, own_ref, positive_ref, totals_ref)
    for j in range(count):
        step = step + refs[j][:rows, :].astype(jnp.int32).astype(F32) * turned[:, j : j + 1]
    step = step * INV_TEMP
    raw = raw_ref[...].astype(F32)
    scale = lax.rsqrt(jnp.mean(raw * raw, axis=-1, keepdims=True) + EPSILON)
    inner = jnp.mean(step * raw, axis=-1, keepdims=True)
    grad_ref[...] = (step - raw * (scale * scale * inner)) * (scale / math.sqrt(raw.shape[1]))


def finish(loss, raw, positive, own, totals, parts):
    return call(
        functools.partial(finish_kernel, len(parts)),
        "finish",
        [jax.ShapeDtypeStruct(own.shape, F32), jax.ShapeDtypeStruct(loss.shape, F32)],
        5e8,
        in_specs=[NEAR] * (5 + len(parts)),
    )(loss, raw, positive, own, totals, *parts)


def on_device(features, patch_index, positive_index, bank):
    groups, copies = lax.axis_size("bank"), lax.axis_size("dp")
    place = lax.axis_index("bank")
    core = lax.axis_index("dp") % 2
    images, hw_dev, channels = features.shape
    queries_dp = images * patch_index.shape[1]
    owned = queries_dp // groups
    turns = groups // 2
    inner, outer = place % 2, place // 2
    bank_dev = bank.shape[0]
    across = [(b, b ^ 1) for b in range(groups)]
    swap = [(c, c ^ 1) for c in range(copies)]

    def turn(value, k):
        pairs = [(b, b ^ (2 * k)) for b in range(groups)]
        return lax.ppermute(value, "bank", pairs)

    def to_all(values):
        return [values[0]] + [turn(values[k], k) for k in [*range(2, turns), 1]]

    cap = capacity(queries_dp / groups / 2, queries_dp // 2, 4.0)
    half = bank_dev // 2
    relay = half * 2 // 8 // 16 * 16
    rest = half - 2 * relay
    row = (lax.axis_index("dp") // 2) % 2
    start = core * half // 16
    numbers = jnp.stack([place, start + row * (relay // 16), start + relay // 8])
    own_set, other_set, relay_out, rest_out = pick(features, patch_index, bank, numbers, relay, rest, owned, cap)
    from_side = lax.ppermute(other_set, "bank", across)
    relayed = lax.ppermute(relay_out, "bank", across)
    rest_in = lax.ppermute(rest_out, "bank", across)
    held_rows = jnp.concatenate([own_set, from_side])
    parts = [held_rows]
    for k in range(1, turns):
        parts.append(turn(parts[k & (k - 1)], k & -k))
    parts = parts[::2] + parts[1::2]

    loc, most = locate(patch_index, place, groups, owned, cap, hw_dev, [from_side])
    over = [(c, c ^ 2) for c in range(copies)]
    from_row = lax.ppermute(after(relayed, loc), "dp", over)

    cap_pos = capacity(queries_dp / groups / 2, queries_dp // 2, 5.0)
    index = positive_index.reshape(images, -1)
    numbers = jnp.stack([place, core, row])
    near_keys, own_keys, listed, key_loc, held = bring_keys(
        index, bank, numbers, groups, owned, cap_pos, relay, [from_side]
    )

    here = place.reshape(1)
    early_rows = early(here, loc, parts[:2], turns, [])
    query, raw, blocks = arrange(here, loc, early_rows, parts[2:], 4 * cap, turns, [near_keys, key_loc])

    far_keys = []
    for part in (relayed, from_row, rest_in):
        part = after(part, query)
        far_keys += [part, lax.ppermute(part, "dp", swap)]
    total, pushed = first(query, near_keys, turns, [far_keys[0], far_keys[2], far_keys[4]])
    note, positive = far_totals(here, key_loc, query, total, own_keys, listed, far_keys, turns)
    came = to_all([note] * turns)
    came = [came[-1], *came[1:-1]]
    loss, totals, word = settle(note, most, held, came, turns, (cap, cap_pos))
    moved = [None] * turns
    order = [*range(2, turns)]
    order.insert(1, 1)
    whole = {k: last(blocks[k], pushed[k], far_keys, note) for k in order[:3]}
    words = [word]
    for axis, step in [("dp", 1), ("bank", 1)] + [("dp", 1 << i) for i in range(1, copies.bit_length() - 1)]:
        pairs = [(i, i ^ step) for i in range(lax.axis_size(axis))]
        came_word = lax.ppermute(words[-1], axis, pairs)
        words.append(words[-1] + came_word)
    gates = [totals]
    for k in order:
        if k not in whole:
            whole[k] = last(blocks[k], pushed[k], far_keys, gates[0])
        sent = code(whole[k], positive[k], totals, k, gates)
        moved[k] = turn(sent, k)
        gates = [sent, words[1]]
    own = last(blocks[0], pushed[0], far_keys, words[-2])
    mean_loss, flag = mean(words[-2], came_word, queries_dp * copies)
    ready = [loss, raw, positive[0], own, totals, *moved[1:]]

    def usual(given, ready, mean_loss):
        grad, loss = finish(*ready[:5], ready[5:])
        return (loss.reshape(owned), grad, mean_loss)

    return lax.cond(
        flag.reshape(()) > 0,
        lambda given, ready, mean_loss: plain(*given),
        usual,
        [features, patch_index, positive_index, bank],
        ready,
        mean_loss.reshape(()),
    )


def solution(mesh):
    in_specs = (P("dp", "bank", None), P("dp", None), P("dp"), P("bank", None))
    out_specs = (P(("dp", "bank")), P(("dp", "bank"), None), P())
    turns = mesh.shape["bank"] // 2
    paired = turns > 2 and turns & (turns - 1) == 0 and mesh.shape["bank"] % 2 == 0
    copies = mesh.shape["dp"]
    paired = paired and copies > 2 and copies & (copies - 1) == 0
    return jax.shard_map(
        on_device if paired else plain, mesh=mesh, in_specs=in_specs, out_specs=out_specs, check_vma=False
    )
```
